32 devices in a mesh: dp: 4 (over y, x), ctx: 8 (over z, core).
Axes of the slice: x: 2, y: 2, z: 4, core: 2. Of those that a mesh axis runs over, the one named last changes fastest.
Arguments:
- inputs: bfloat16 [2, 4, 1024, 576], P(None, 'dp', 'ctx'), may hold values from -6 to 6
- norm_gains: float32 [2, 576], P(None, 'ctx'), may hold values from 0.5 to 1.5
- w_query: bfloat16 [331776], P(('dp', 'ctx')), may hold values from -0.25 to 0.25
- w_key: bfloat16 [110592], P(('dp', 'ctx')), may hold values from -0.25 to 0.25
- w_value: bfloat16 [110592], P(('dp', 'ctx')), may hold values from -0.25 to 0.25
- w_output: bfloat16 [331776], P(('dp', 'ctx')), may hold values from -6 to 6
- w_gate: bfloat16 [884736], P(('dp', 'ctx')), may hold values from -0.25 to 0.25
- w_up: bfloat16 [884736], P(('dp', 'ctx')), may hold values from -0.25 to 0.25
- w_down: bfloat16 [884736], P(('dp', 'ctx')), may hold values from -0.15625 to 0.15625
- cotangent: bfloat16 [2, 4, 1024, 576], P(None, 'dp', 'ctx'), may hold values from -6 to 6
Outputs:
- result: bfloat16 [2, 4, 1024, 576], P(None, 'dp', 'ctx')
- grad_inputs: bfloat16 [2, 4, 1024, 576], P(None, 'dp', 'ctx')
- grad_gains: float32 [2, 576], P(None, 'ctx')
- grad_query: float32 [331776], P(('dp', 'ctx'))
- grad_key: float32 [110592], P(('dp', 'ctx'))
- grad_value: float32 [110592], P(('dp', 'ctx'))
- grad_output: float32 [331776], P(('dp', 'ctx'))
- grad_gate: float32 [884736], P(('dp', 'ctx'))
- grad_up: float32 [884736], P(('dp', 'ctx'))
- grad_down: float32 [884736], P(('dp', 'ctx'))
The draws below stay inside these ranges and needn't reach their ends.
All inputs are finite; a program needn't handle non-finite values.
Results may differ from the reference program's by a relative error of at most 0.014.
Values may be sent and summed in bfloat16 or wider, within the bound.
A program may use at most 128 MiB of HBM per device.

```python
import jax
import jax.numpy as jnp
from jax import lax

D = 576
H = 9
KV = 3
HD = 64
FF = 1536
MB = 2
SEQS = 4
SEQ_LEN = 1024


def steps_of(key, dims, shards, least, top_value):
    loudness = 1.0
    for position, shards_of in shards:
        draws = jax.random.uniform(jax.random.fold_in(jax.random.fold_in(key, 6), position), (shards_of,), jnp.float32, least / len(shards), top_value / len(shards))
        loudness = loudness * jnp.repeat(jnp.exp(draws), dims[position] // shards_of).reshape((-1,) + (1,) * (len(dims) - 1 - position))
    return loudness


def centred(key, dims, spread, limit, cuts=(), held_as=jnp.bfloat16):
    result = spread * jax.random.normal(key, dims, jnp.float32)
    if cuts:
        result = result * steps_of(key, dims, cuts, -0.22, 0.18)
    return jnp.clip(result, -limit, limit).astype(held_as)


def setup_inputs(seed: int = 0) -> dict:
    seeds = jax.random.split(jax.random.key(seed), 11)
    return {
        "inputs": centred(seeds[0], (MB, SEQS, SEQ_LEN, D), 1.0, 6.0, ((1, 4), (2, 8))),
        "norm_gains": jnp.clip(1.0 + 0.1 * jax.random.normal(seeds[1], (2, D), jnp.float32), 0.5, 1.5),
        "w_query": centred(seeds[2], (D * H * HD,), D ** -0.5, 0.25, ((0, 32),)),
        "w_key": centred(seeds[3], (D * KV * HD,), D ** -0.5, 0.25, ((0, 32),)),
        "w_value": centred(seeds[4], (D * KV * HD,), D ** -0.5, 0.25, ((0, 32),)),
        "w_output": centred(seeds[5], (H * HD * D,), (max(1, D * 3 // SEQ_LEN)) ** -0.5, 6.0, ((0, 32),)),
        "w_gate": centred(seeds[6], (D * FF,), D ** -0.5, 0.25, ((0, 32),)),
        "w_up": centred(seeds[7], (D * FF,), D ** -0.5, 0.25, ((0, 32),)),
        "w_down": centred(seeds[8], (FF * D,), FF ** -0.5, 0.15625, ((0, 32),)),
        "cotangent": centred(seeds[9], (MB, SEQS, SEQ_LEN, D), 1.0, 6.0, ((1, 4), (2, 8))),
    }


eps = 1e-05
rope_base = 10000.0
score_scale = 0.125
big_negative = -1e+30

@jax.custom_vjp
def low(v):
    return lax.optimization_barrier(v.astype(jnp.bfloat16)).astype(jnp.float32)

@jax.custom_vjp
def low_back(v):
    return v

def low_keep(v):
    return (low(v), None)

def low_pass(kept, grad):
    return (grad,)

def back_keep(v):
    return (v, None)

def back_low(kept, grad):
    return (low(grad),)
low.defvjp(low_keep, low_pass)
low_back.defvjp(back_keep, back_low)

def highest(left_side, right_side):
    return jnp.dot(left_side, right_side, precision=lax.Precision.HIGHEST)

def rms_scale(values):
    return lax.rsqrt(lax.optimization_barrier(jnp.mean(values * values, axis=-1, keepdims=True)) + eps)

def rope_tables(positions):
    half_size = HD // 2
    frequency = rope_base ** (-jnp.arange(half_size, dtype=jnp.float32) / half_size)
    angles = positions.astype(jnp.float32)[:, None] * frequency[None, :]
    return (jnp.cos(angles), jnp.sin(angles))

def rotate(values, cosine, sine_table, head_count):
    row_count = values.shape[0]
    shaped = values.reshape(row_count, head_count, 2, HD // 2)
    first_half = shaped[:, :, 0, :]
    second_half = shaped[:, :, 1, :]
    cos_rows = cosine[:, None, :]
    sin_rows = sine_table[:, None, :]
    turned = jnp.stack([first_half * cos_rows - second_half * sin_rows, second_half * cos_rows + first_half * sin_rows], axis=2)
    return turned.reshape(row_count, head_count * HD)

def attention(queries, key_rows, value_rows):
    seq_length = queries.shape[0]
    query_block = min(512, seq_length)
    grouped_keys = key_rows.reshape(seq_length, KV, HD)
    grouped_values = value_rows.reshape(seq_length, KV, HD)
    key_pos = jnp.arange(seq_length, dtype=jnp.int32)

    def one_block(block_index):
        first = (block_index * query_block).astype(jnp.int32)
        rows_here = lax.dynamic_slice_in_dim(queries, first, query_block, 0).reshape(query_block, KV, H // KV, HD)
        scores = low_back(jnp.einsum('qkgd,nkd->kgqn', rows_here, grouped_keys, precision=lax.Precision.HIGHEST))
        query_pos = first + jnp.arange(query_block, dtype=jnp.int32)
        visible = key_pos[None, :] <= query_pos[:, None]
        probs = jax.nn.softmax(jnp.where(visible, scores, big_negative), axis=-1)
        mixed_rows = jnp.einsum('kgqn,nkd->qkgd', low(probs), grouped_values, precision=lax.Precision.HIGHEST)
        return mixed_rows.reshape(query_block, H * HD)
    pieces = lax.map(jax.checkpoint(one_block), jnp.arange(seq_length // query_block, dtype=jnp.int32))
    return pieces.reshape(seq_length, H * HD)

def layer(x_float, gains, matrices):
    query_mat, key_mat, value_mat, output_mat, gate_mat, up_mat, down_mat = matrices
    seq_length = x_float.shape[0]
    cosine, sine_table = rope_tables(jnp.arange(seq_length, dtype=jnp.int32))
    normed_one = low(x_float * rms_scale(x_float) * gains[0])
    queries = low(rotate(low_back(highest(normed_one, query_mat)), cosine, sine_table, H) * score_scale)
    key_rows = low(rotate(low_back(highest(normed_one, key_mat)), cosine, sine_table, KV))
    value_rows = low(low_back(highest(normed_one, value_mat)))
    attended = low(low_back(attention(queries, key_rows, value_rows)))
    residual = x_float + low_back(highest(attended, output_mat))
    normed_two = low(residual * rms_scale(residual) * gains[1])
    gate_pre = low_back(highest(normed_two, gate_mat))
    up_pre = low_back(highest(normed_two, up_mat))
    activated = low(jax.nn.silu(gate_pre) * up_pre)
    return residual + low_back(highest(activated, down_mat))

def reference(inputs, norm_gains, w_query, w_key, w_value, w_output, w_gate, w_up, w_down, cotangent):
    micro_count, seq_count, seq_length, width = inputs.shape
    total_seqs = micro_count * seq_count
    flat_inputs = inputs.reshape(total_seqs, seq_length, width)
    flat_cotangent = cotangent.reshape(total_seqs, seq_length, width)
    matrices = (w_query.astype(jnp.float32).reshape(D, H * HD), w_key.astype(jnp.float32).reshape(D, KV * HD), w_value.astype(jnp.float32).reshape(D, KV * HD), w_output.astype(jnp.float32).reshape(H * HD, D), w_gate.astype(jnp.float32).reshape(D, FF), w_up.astype(jnp.float32).reshape(D, FF), w_down.astype(jnp.float32).reshape(FF, D))
    gains = norm_gains.astype(jnp.float32)

    def one_sequence(totals, pair):
        seq_inputs, seq_cotangent = pair
        outcome, pullback = jax.vjp(layer, seq_inputs.astype(jnp.float32), gains, matrices)
        grad_x, grad_g, grad_mats = pullback(seq_cotangent.astype(jnp.float32))
        updated = (totals[0] + grad_g, jax.tree.map(jnp.add, totals[1], grad_mats))
        return (updated, (outcome.astype(jnp.bfloat16), grad_x.astype(jnp.bfloat16)))
    zero_totals = (jnp.zeros_like(gains), jax.tree.map(jnp.zeros_like, matrices))
    totals, stacked = lax.scan(one_sequence, zero_totals, (flat_inputs, flat_cotangent))
    grad_mats = totals[1]
    return (stacked[0].reshape(inputs.shape), stacked[1].reshape(inputs.shape), totals[0], grad_mats[0].reshape(-1), grad_mats[1].reshape(-1), grad_mats[2].reshape(-1), grad_mats[3].reshape(-1), grad_mats[4].reshape(-1), grad_mats[5].reshape(-1), grad_mats[6].reshape(-1))
```

```python
import functools
import jax
import jax.numpy as jnp
from jax import lax
from jax.experimental import pallas as pl
from jax.experimental.pallas import tpu as pltpu
from jax.sharding import PartitionSpec as P

D = 576
H = 9
KV = 3
HD = 64
FF = 1536


eps = 1e-05
rope_base = 10000.0
score_scale = 0.125
big_negative = -1e30


def rms_scale(values):
    return lax.rsqrt(jnp.mean(values * values, axis=-1, keepdims=True) + eps)


def norm_back(grad_out, values, row_scale, gain_row):
    weighted = grad_out * gain_row
    cubed = row_scale * row_scale * row_scale
    return row_scale * weighted - values * cubed * jnp.mean(
        weighted * values, axis=-1, keepdims=True
    )


def rope_tables(positions):
    half_size = HD // 2
    frequency = rope_base ** (-jnp.arange(half_size, dtype=jnp.float32) / half_size)
    angles = positions.astype(jnp.float32)[:, None] * frequency[None, :]
    return (jnp.cos(angles), jnp.sin(angles))


def rotate(values, cosine, sine_table, head_count, direction):
    row_count = values.shape[0]
    shaped = values.reshape(row_count, head_count, 2, HD // 2)
    first_half = shaped[:, :, 0, :]
    second_half = shaped[:, :, 1, :]
    cos_rows = cosine[:, None, :]
    sin_rows = direction * sine_table[:, None, :]
    turned = jnp.stack(
        [
            first_half * cos_rows - second_half * sin_rows,
            second_half * cos_rows + first_half * sin_rows,
        ],
        axis=2,
    )
    return turned.reshape(row_count, head_count * HD)


def across_rows(left_side, right_side):
    return lax.dot_general(
        left_side, right_side, (((0,), (0,)), ((), ())), preferred_element_type=jnp.float32
    )


def against(left_side, right_side):
    return lax.dot_general(
        left_side, right_side, (((1,), (1,)), ((), ())), preferred_element_type=jnp.float32
    )


def unpack(gathered, piece_sizes):
    mat_shapes = ((D, H * HD), (D, KV * HD), (D, KV * HD), (H * HD, D), (D, FF), (D, FF), (FF, D))
    matrices = []
    offset = 0
    for piece_len, mat_shape in zip(piece_sizes, mat_shapes):
        matrices.append(gathered[:, offset : offset + piece_len].reshape(mat_shape))
        offset = offset + piece_len
    return tuple(matrices)


def block_scores(queries, gathered_kv, block_index, key_block, first_row):
    row_count = queries.shape[0]
    key_rows = lax.dynamic_slice_in_dim(gathered_kv, block_index * key_block, key_block, 0)
    key_part = key_rows[:, : KV * HD].reshape(key_block, KV, HD)
    value_part = key_rows[:, KV * HD :].reshape(key_block, KV, HD)
    grouped = queries.reshape(row_count, KV, H // KV, HD)
    scores = jnp.einsum("qkgd,nkd->kgqn", grouped, key_part, preferred_element_type=jnp.float32)
    query_pos = first_row + jnp.arange(row_count)
    key_pos = block_index * key_block + jnp.arange(key_block)
    visible = key_pos[None, :] <= query_pos[:, None]
    return (scores, visible, key_part, value_part, grouped)


def attend(queries, gathered_kv, first_row, key_block, block_count):
    row_count = queries.shape[0]
    group_size = H // KV

    def running(block_index, state_pair):
        row_max, row_total = state_pair
        scores, visible, key_part, value_part, grouped = block_scores(
            queries, gathered_kv, block_index, key_block, first_row
        )
        masked = jnp.where(visible, scores, big_negative)
        new_max = jnp.maximum(row_max, jnp.max(masked, axis=-1))
        weights = jnp.where(visible, jnp.exp(masked - new_max[..., None]), 0.0)
        return (new_max, row_total * jnp.exp(row_max - new_max) + jnp.sum(weights, axis=-1))

    initial = (
        jnp.full((KV, group_size, row_count), big_negative, jnp.float32),
        jnp.zeros((KV, group_size, row_count), jnp.float32),
    )
    row_max, row_total = lax.fori_loop(0, block_count, running, initial)
    log_total = row_max + jnp.log(row_total)

    def weighted_sum(block_index, accum):
        scores, visible, key_part, value_part, grouped = block_scores(
            queries, gathered_kv, block_index, key_block, first_row
        )
        weights_low = jnp.where(visible, jnp.exp(scores - log_total[..., None]), 0.0).astype(
            jnp.bfloat16
        )
        return accum + jnp.einsum(
            "kgqn,nkd->qkgd", weights_low, value_part, preferred_element_type=jnp.float32
        )

    attn_mixed = lax.fori_loop(
        0, block_count, weighted_sum, jnp.zeros((row_count, KV, group_size, HD), jnp.float32)
    )
    return (attn_mixed.reshape(row_count, H * HD), log_total)


def attend_back(
    queries, gathered_kv, first_row, key_block, block_count, log_total, grad_grouped, delta
):
    row_count = queries.shape[0]
    group_size = H // KV

    def back_step(block_index, grad_query):
        scores, visible, key_part, value_part, grouped = block_scores(
            queries, gathered_kv, block_index, key_block, first_row
        )
        weights = jnp.where(visible, jnp.exp(scores - log_total[..., None]), 0.0)
        grad_weights = jnp.einsum(
            "qkgd,nkd->kgqn", grad_grouped, value_part, preferred_element_type=jnp.float32
        )
        grad_scores = (weights * (grad_weights - delta[..., None])).astype(jnp.bfloat16)
        return grad_query + jnp.einsum(
            "kgqn,nkd->qkgd", grad_scores, key_part, preferred_element_type=jnp.float32
        )

    grad_query = lax.fori_loop(
        0, block_count, back_step, jnp.zeros((row_count, KV, group_size, HD), jnp.float32)
    )
    return grad_query.reshape(row_count, H * HD)


def key_side(own_keys, own_values, key_first, stats, carry, pieces):
    query_piece, grad_piece = pieces
    lse_all, delta_all = stats
    piece_rows = query_piece.shape[0]
    block_rows = min(512, piece_rows)
    group_size = H // KV
    own_count = own_keys.shape[0]
    key_pos = key_first + jnp.arange(own_count, dtype=jnp.int32)

    def block_step(accums, block_index):
        grad_key, grad_value = accums
        row_start = block_index * block_rows
        query_block = lax.dynamic_slice_in_dim(query_piece, row_start, block_rows, 0).reshape(
            block_rows, KV, group_size, HD
        )
        grad_block = lax.dynamic_slice_in_dim(grad_piece, row_start, block_rows, 0).reshape(
            block_rows, KV, group_size, HD
        )
        lse_block = lax.dynamic_slice_in_dim(lse_all, row_start, block_rows, 1).reshape(
            KV, group_size, block_rows
        )
        delta_block = lax.dynamic_slice_in_dim(delta_all, row_start, block_rows, 1).reshape(
            KV, group_size, block_rows
        )
        scores = jnp.einsum(
            "qkgd,nkd->kgqn", query_block, own_keys, preferred_element_type=jnp.float32
        )
        query_pos = row_start + jnp.arange(block_rows, dtype=jnp.int32)
        visible = key_pos[None, :] <= query_pos[:, None]
        weights = jnp.where(visible, jnp.exp(scores - lse_block[..., None]), 0.0)
        grad_value = grad_value + jnp.einsum(
            "kgqn,qkgd->nkd",
            weights.astype(jnp.bfloat16),
            grad_block,
            preferred_element_type=jnp.float32,
        )
        grad_weights = jnp.einsum(
            "qkgd,nkd->kgqn", grad_block, own_values, preferred_element_type=jnp.float32
        )
        grad_scores = (weights * (grad_weights - delta_block[..., None])).astype(jnp.bfloat16)
        grad_key = grad_key + jnp.einsum(
            "kgqn,qkgd->nkd", grad_scores, query_block, preferred_element_type=jnp.float32
        )
        return ((grad_key, grad_value), None)

    outcome, ignored = lax.scan(
        block_step, carry, jnp.arange(piece_rows // block_rows, dtype=jnp.int32)
    )
    return outcome


def on_device(
    inputs, norm_gains, w_query, w_key, w_value, w_output, w_gate, w_up, w_down, cotangent
):
    ctx_size = lax.axis_size("ctx")
    device_count = lax.axis_size("dp") * ctx_size
    row_count = inputs.shape[2]
    seq_length = row_count * ctx_size
    first_row = lax.axis_index("ctx") * row_count
    key_block = min(512, seq_length)
    block_count = (first_row + row_count - 1) // key_block + 1
    group_size = H // KV
    cosine, sine_table = rope_tables(first_row + jnp.arange(row_count))
    weight_flats = (w_query, w_key, w_value, w_output, w_gate, w_up, w_down)
    piece_sizes = [flat_piece.shape[0] for flat_piece in weight_flats]
    packed = jnp.concatenate([flat_piece.reshape(1, -1) for flat_piece in weight_flats], axis=1)
    saved_rows = []
    out_rows = []
    grad_rows = []
    gain_terms = []
    for micro_batch in range(inputs.shape[0]):
        matrices = unpack(lax.all_gather(packed, ("dp", "ctx"), axis=0, tiled=True), piece_sizes)
        gain_rows = lax.all_gather(norm_gains, "ctx", axis=1, tiled=True)
        query_mat, key_mat, value_mat, output_mat, gate_mat, up_mat, down_mat = matrices
        x_float = inputs[micro_batch, 0].astype(jnp.float32)
        scale_one = rms_scale(x_float)
        normed_one = (x_float * scale_one * gain_rows[0]).astype(jnp.bfloat16)
        queries = (
            rotate(
                jnp.dot(normed_one, query_mat, preferred_element_type=jnp.float32),
                cosine,
                sine_table,
                H,
                1.0,
            )
            * score_scale
        ).astype(jnp.bfloat16)
        key_rows = rotate(
            jnp.dot(normed_one, key_mat, preferred_element_type=jnp.float32),
            cosine,
            sine_table,
            KV,
            1.0,
        ).astype(jnp.bfloat16)
        value_rows = jnp.dot(normed_one, value_mat, preferred_element_type=jnp.float32).astype(
            jnp.bfloat16
        )
        gathered_kv = lax.all_gather(
            jnp.concatenate([key_rows, value_rows], axis=1), "ctx", axis=0, tiled=True
        )
        attn_mixed, log_total = attend(queries, gathered_kv, first_row, key_block, block_count)
        attended = attn_mixed.astype(jnp.bfloat16)
        residual = x_float + jnp.dot(attended, output_mat, preferred_element_type=jnp.float32)
        scale_two = rms_scale(residual)
        normed_two = (residual * scale_two * gain_rows[1]).astype(jnp.bfloat16)
        gate_pre = jnp.dot(normed_two, gate_mat, preferred_element_type=jnp.float32)
        up_pre = jnp.dot(normed_two, up_mat, preferred_element_type=jnp.float32)
        gate_sig = jax.nn.sigmoid(gate_pre)
        swish_val = gate_pre * gate_sig
        activated = (swish_val * up_pre).astype(jnp.bfloat16)
        outcome = residual + jnp.dot(activated, down_mat, preferred_element_type=jnp.float32)
        out_rows.append(outcome.astype(jnp.bfloat16))
        query_back, key_back, value_back, output_back, gate_back, up_back, down_back = matrices
        grad_out = cotangent[micro_batch, 0]
        grad_act = against(grad_out, down_back)
        grad_gate_pre = (grad_act * up_pre * gate_sig * (1.0 + gate_pre * (1.0 - gate_sig))).astype(
            jnp.bfloat16
        )
        grad_up_pre = (grad_act * swish_val).astype(jnp.bfloat16)
        grad_norm_two = against(grad_gate_pre, gate_back) + against(grad_up_pre, up_back)
        gain_two = jnp.sum(grad_norm_two * residual * scale_two, axis=0)
        grad_residual = grad_out.astype(jnp.float32) + norm_back(
            grad_norm_two, residual, scale_two, gain_rows[1]
        )
        grad_branch = grad_residual.astype(jnp.bfloat16)
        grad_attn = against(grad_branch, output_back).astype(jnp.bfloat16)
        grad_grouped = grad_attn.reshape(row_count, KV, group_size, HD)
        product = (grad_attn.astype(jnp.float32) * attn_mixed).reshape(
            row_count, KV, group_size, HD
        )
        delta = jnp.transpose(jnp.sum(product, axis=-1), (1, 2, 0))
        grad_query = attend_back(
            queries, gathered_kv, first_row, key_block, block_count, log_total, grad_grouped, delta
        )
        stats = (
            lax.all_gather(log_total.reshape(H, row_count), "ctx", axis=1, tiled=True),
            lax.all_gather(delta.reshape(H, row_count), "ctx", axis=1, tiled=True),
        )
        own_keys = key_rows.reshape(row_count, KV, HD)
        own_values = value_rows.reshape(row_count, KV, HD)
        zero_rows = jnp.zeros((row_count, KV, HD), jnp.float32)
        grad_key_sum, grad_value_sum = key_side(
            own_keys,
            own_values,
            first_row,
            stats,
            (zero_rows, zero_rows),
            (
                lax.all_gather(queries, "ctx", axis=0, tiled=True),
                lax.all_gather(grad_attn, "ctx", axis=0, tiled=True),
            ),
        )
        grad_q_low = (rotate(grad_query, cosine, sine_table, H, -1.0) * score_scale).astype(
            jnp.bfloat16
        )
        grad_k_low = rotate(
            grad_key_sum.reshape(row_count, KV * HD), cosine, sine_table, KV, -1.0
        ).astype(jnp.bfloat16)
        grad_v_low = grad_value_sum.reshape(row_count, KV * HD).astype(jnp.bfloat16)
        grad_norm_one = (
            against(grad_q_low, query_back)
            + against(grad_k_low, key_back)
            + against(grad_v_low, value_back)
        )
        gain_one = jnp.sum(grad_norm_one * x_float * scale_one, axis=0)
        grad_x = grad_residual + norm_back(grad_norm_one, x_float, scale_one, gain_rows[0])
        grad_rows.append(grad_x.astype(jnp.bfloat16))
        gain_terms.append(jnp.stack([gain_one, gain_two], axis=0))
        saved_rows.append(
            (
                normed_one,
                grad_q_low,
                grad_k_low,
                grad_v_low,
                attended,
                grad_branch,
                normed_two,
                grad_gate_pre,
                grad_up_pre,
                activated,
                grad_out,
            )
        )
    joined = [
        jnp.concatenate([saved_set[member] for saved_set in saved_rows], axis=0)
        for member in range(11)
    ]
    local_grads = (
        across_rows(joined[0], joined[1]),
        across_rows(joined[0], joined[2]),
        across_rows(joined[0], joined[3]),
        across_rows(joined[4], joined[5]),
        across_rows(joined[6], joined[7]),
        across_rows(joined[6], joined[8]),
        across_rows(joined[9], joined[10]),
    )
    grad_table = jnp.concatenate(
        [grad_mat.reshape(device_count, -1) for grad_mat in local_grads], axis=1
    )
    owned = lax.psum_scatter(grad_table, ("dp", "ctx"), scatter_dimension=0, tiled=True)
    owned_parts = []
    offset = 0
    for piece_len in piece_sizes:
        owned_parts.append(owned[0, offset : offset + piece_len])
        offset = offset + piece_len
    gain_local = gain_terms[0]
    for extra_term in gain_terms[1:]:
        gain_local = gain_local + extra_term
    gain_total = lax.psum(gain_local, ("dp", "ctx"))
    gain_width = D // ctx_size
    gain_share = lax.dynamic_slice_in_dim(
        gain_total, lax.axis_index("ctx") * gain_width, gain_width, 1
    )
    return (
        jnp.stack(out_rows)[:, None],
        jnp.stack(grad_rows)[:, None],
        gain_share,
        owned_parts[0],
        owned_parts[1],
        owned_parts[2],
        owned_parts[3],
        owned_parts[4],
        owned_parts[5],
        owned_parts[6],
    )


def general_solution(mesh):
    placed = (
        P(None, "dp", "ctx", None),
        P(None, "ctx"),
        P(("dp", "ctx")),
        P(("dp", "ctx")),
        P(("dp", "ctx")),
        P(("dp", "ctx")),
        P(("dp", "ctx")),
        P(("dp", "ctx")),
        P(("dp", "ctx")),
        P(None, "dp", "ctx", None),
    )
    return jax.shard_map(
        on_device,
        mesh=mesh,
        in_specs=placed,
        out_specs=(
            P(None, "dp", "ctx", None),
            P(None, "dp", "ctx", None),
            P(None, "ctx"),
            P(("dp", "ctx")),
            P(("dp", "ctx")),
            P(("dp", "ctx")),
            P(("dp", "ctx")),
            P(("dp", "ctx")),
            P(("dp", "ctx")),
            P(("dp", "ctx")),
        ),
        check_vma=False,
    )


BF = jnp.bfloat16
F32 = jnp.float32
MESH = pl.DeviceIdType.MESH
MAIN = 16
PACK = 768


def place():
    dp_at = lax.axis_index("dp")
    ctx_at = lax.axis_index("ctx")
    core = lax.rem(ctx_at, 2)
    flip_one = dp_at + 1 - 2 * lax.rem(dp_at, 2)
    flip_two = lax.rem(dp_at + 2, 4)
    first = (1 - core) * flip_one + core * flip_two
    second = (1 - core) * flip_two + core * flip_one
    return (dp_at, ctx_at, core, ctx_at // 2, first, second, 3 - dp_at)


def greet(targets):
    barrier = pltpu.get_barrier_semaphore()
    for target in targets:
        pl.semaphore_signal(barrier, inc=1, device_id=target, device_id_type=MESH)
    pl.semaphore_wait(barrier, len(targets))


def rows(index, size):
    return pl.ds(pl.multiple_of(index * size, size), size)


def remote(src, dst, send, recv, target):
    return pltpu.make_async_remote_copy(
        src_ref=src, dst_ref=dst, send_sem=send, recv_sem=recv, device_id=target, device_id_type=MESH
    )


def tail_matrix(shards, transposed):
    width = shards * MAIN
    shape = (width, 384) if transposed else (384, width)
    out_at = lax.broadcasted_iota(jnp.int32, shape, 1 if transposed else 0)
    in_at = lax.broadcasted_iota(jnp.int32, shape, 0 if transposed else 1)
    wanted = (lax.rem(out_at, 64) // 2) * MAIN + (out_at // 64) * 2 + lax.rem(out_at, 2)
    return jnp.where(wanted == in_at, 1.0, 0.0).astype(BF)


def gather_weights_kernel(
    ctx_size, w_ref, d_ref, t_ref, ow_ref, od_ref, og_ref, tg_ref, send, recv
):
    dp_at, ctx_at, core, z_at, first, second, across = place()
    depth = ctx_size // 2
    shards = 4 * ctx_size
    sibling = (dp_at, ctx_at + 1 - 2 * core)
    to_first = (first, ctx_at)
    to_second = (second, ctx_at)
    z_peers = [(dp_at, 2 * lax.rem(z_at + i, depth) + core) for i in range(1, depth)]
    greet(z_peers + [to_first, to_second, sibling])
    me = dp_at * ctx_size + ctx_at
    ow_ref[:, rows(me, 16), :] = w_ref[...]
    od_ref[rows(me, 48), :] = d_ref[...]
    tg_ref[rows(me, 16), :] = t_ref[...]
    sent = []

    def copies(shard, target, slot):
        return [
            remote(part, part, send.at[slot, k], recv.at[shard, k], target)
            for k, part in enumerate(
                (
                    ow_ref.at[:, rows(shard, 16), :],
                    od_ref.at[rows(shard, 48), :],
                    tg_ref.at[rows(shard, 16), :],
                )
            )
        ]

    def push(shard, targets):
        for target in targets:
            group = copies(shard, target, len(sent))
            for one in group:
                one.start()
            sent.append(group)

    def arrive(shard):
        for one in copies(shard, sibling, 0):
            one.wait_recv()

    push(me, z_peers + [to_first, to_second, sibling])
    back = [lax.rem(z_at + depth - i, depth) for i in range(depth)]
    for z_from in back[1:]:
        shard = dp_at * ctx_size + 2 * z_from + core
        arrive(shard)
        push(shard, [to_first, to_second, sibling])
    for z_from in back:
        shard = first * ctx_size + 2 * z_from + core
        arrive(shard)
        push(shard, [to_second, sibling])
        shard = second * ctx_size + 2 * z_from + core
        arrive(shard)
        push(shard, [sibling])
    for z_from in back:
        shard = across * ctx_size + 2 * z_from + core
        arrive(shard)
        push(shard, [sibling])
    for dp_from in (dp_at, first, second, across):
        for z_from in back:
            arrive(dp_from * ctx_size + 2 * z_from + 1 - core)
    for group in sent:
        for one in group:
            one.wait_send()
    unpacked = jnp.dot(
        tail_matrix(shards, False), tg_ref[...], preferred_element_type=F32
    ).astype(BF)
    for part in range(6):
        ow_ref[part // 2, 512:576, (part % 2) * PACK : (part % 2 + 1) * PACK] = unpacked[
            64 * part : 64 * part + 64
        ]
    og_ref[...] = tg_ref[0 : ctx_size * 16, :]


def vmem_specs(count):
    return [pl.BlockSpec(memory_space=pltpu.VMEM)] * count


def gather_weights(ctx_size, w_main, w_low, w_tail):
    shards = 4 * ctx_size
    return pl.pallas_call(
        functools.partial(gather_weights_kernel, ctx_size),
        out_shape=(
            jax.ShapeDtypeStruct((3, D, FF), BF),
            jax.ShapeDtypeStruct((FF, D), BF),
            jax.ShapeDtypeStruct((ctx_size * 16, PACK), BF),
        ),
        in_specs=vmem_specs(3),
        out_specs=tuple(vmem_specs(3)),
        scratch_shapes=[
            pltpu.VMEM((shards * 16, PACK), BF),
            pltpu.SemaphoreType.DMA((shards, 3)),
            pltpu.SemaphoreType.DMA((shards, 3)),
        ],
        compiler_params=pltpu.CompilerParams(
            collective_id=0, has_side_effects=True, vmem_limit_bytes=48 * 1024 * 1024
        ),
        name="gather_weights",
    )(w_main, w_low, w_tail)


def scatter_grads_kernel(
    ctx_size,
    gw_ref,
    gd_ref,
    gx_ref,
    ow_ref,
    od_ref,
    ot_ref,
    tail,
    cw,
    cd,
    ct,
    aw,
    ad,
    at,
    bw,
    bd,
    bt,
    ew,
    ed,
    et,
    zw,
    zd,
    zt,
    send_c,
    recv_c,
    send_d,
    recv_d,
    send_z,
    recv_z,
):
    dp_at, ctx_at, core, z_at, first, second, across = place()
    depth = ctx_size // 2
    shards = 4 * ctx_size
    sibling = (dp_at, ctx_at + 1 - 2 * core)
    to_first = (first, ctx_at)
    to_second = (second, ctx_at)
    order = [lax.rem(z_at + i, depth) for i in range(1, depth + 1)]
    z_peers = [(dp_at, 2 * z_to + core) for z_to in order[:-1]]
    greet(z_peers + [to_first, to_second, sibling])
    stacked = jnp.concatenate(
        [
            gw_ref[part // 2, 512:576, (part % 2) * PACK : (part % 2 + 1) * PACK]
            for part in range(6)
        ],
        axis=0,
    )
    spread = jnp.dot(tail_matrix(shards, True), stacked, preferred_element_type=F32)
    for block in range(4):
        part = slice(block * ctx_size * 16, (block + 1) * ctx_size * 16)
        tail[part, :] = (spread[part] + gx_ref[...].astype(F32)).astype(BF)

    def views(refs, index):
        return (
            refs[0].at[:, rows(index, 16), :],
            refs[1].at[rows(index, 48), :],
            refs[2].at[rows(index, 16), :],
        )

    own = (gw_ref, gd_ref, tail)
    paired = (cw, cd, ct)
    via = (aw, ad, at)
    from_first = (bw, bd, bt)
    from_second = (ew, ed, et)
    along = (zw, zd, zt)
    sent = []

    def ship(src, dst, send, recv, target):
        group = [
            remote(src[k], dst[k], send.at[k], recv.at[k], target) for k in range(3)
        ]
        for one in group:
            one.start()
        sent.append(group)

    def arrive(dst, recv):
        for k in range(3):
            remote(dst[k], dst[k], recv.at[k], recv.at[k], sibling).wait_recv()

    def add(dst, terms):
        for k in range(3):
            total = dst[k][...].astype(F32)
            for term in terms:
                total = total + term[k][...].astype(F32)
            dst[k][...] = total.astype(BF)

    for z_to in order:
        for dp_to in (across, second, first, dp_at):
            shard = dp_to * ctx_size + 2 * z_to + 1 - core
            slot = dp_to * depth + z_to
            ship(views(own, shard), views(paired, slot), send_c.at[slot], recv_c.at[slot], sibling)

    def pair_up(dp_to, z_to):
        slot = dp_to * depth + z_to
        arrive(views(paired, slot), recv_c.at[slot])
        add(views(paired, slot), [views(own, dp_to * ctx_size + 2 * z_to + core)])
        return views(paired, slot)

    for z_to in order:
        partial = pair_up(across, z_to)
        ship(partial, views(via, z_to), send_d.at[0, z_to], recv_d.at[0, z_to], to_second)
        partial = pair_up(second, z_to)
        ship(partial, views(from_second, z_to), send_d.at[1, z_to], recv_d.at[1, z_to], to_second)
        pair_up(first, z_to)
        pair_up(dp_at, z_to)
    for z_to in order:
        partial = views(paired, first * depth + z_to)
        arrive(views(via, z_to), recv_d.at[0, z_to])
        add(partial, [views(via, z_to)])
        ship(partial, views(from_first, z_to), send_d.at[2, z_to], recv_d.at[2, z_to], to_first)
    for number, z_to in enumerate(order):
        partial = views(paired, dp_at * depth + z_to)
        arrive(views(from_second, z_to), recv_d.at[1, z_to])
        arrive(views(from_first, z_to), recv_d.at[2, z_to])
        add(partial, [views(from_second, z_to), views(from_first, z_to)])
        if number < depth - 1:
            ship(
                partial,
                views(along, z_at),
                send_z.at[z_to],
                recv_z.at[z_at],
                (dp_at, 2 * z_to + core),
            )
    for z_from in order[:-1]:
        arrive(views(along, z_from), recv_z.at[z_from])
    for k, out in enumerate((ow_ref, od_ref, ot_ref)):
        total = views(paired, dp_at * depth + z_at)[k][...].astype(F32)
        for z_from in order[:-1]:
            total = total + views(along, z_from)[k][...].astype(F32)
        out[...] = total
    for group in sent:
        for one in group:
            one.wait_send()


def scatter_grads(ctx_size, grad_main, grad_low, gain_rows):
    depth = ctx_size // 2

    def slots(count):
        return [
            pltpu.VMEM((3, count * 16, FF), BF),
            pltpu.VMEM((count * 48, D), BF),
            pltpu.VMEM((count * 16, PACK), BF),
        ]

    return pl.pallas_call(
        functools.partial(scatter_grads_kernel, ctx_size),
        out_shape=(
            jax.ShapeDtypeStruct((3, 16, FF), F32),
            jax.ShapeDtypeStruct((48, D), F32),
            jax.ShapeDtypeStruct((16, PACK), F32),
        ),
        in_specs=vmem_specs(3),
        out_specs=tuple(vmem_specs(3)),
        scratch_shapes=[pltpu.VMEM((4 * ctx_size * 16, PACK), BF)]
        + slots(4 * depth)
        + slots(depth)
        + slots(depth)
        + slots(depth)
        + slots(depth)
        + [
            pltpu.SemaphoreType.DMA((4 * depth, 3)),
            pltpu.SemaphoreType.DMA((4 * depth, 3)),
            pltpu.SemaphoreType.DMA((3, depth, 3)),
            pltpu.SemaphoreType.DMA((3, depth, 3)),
            pltpu.SemaphoreType.DMA((depth, 3)),
            pltpu.SemaphoreType.DMA((depth, 3)),
        ],
        compiler_params=pltpu.CompilerParams(
            collective_id=1, has_side_effects=True, vmem_limit_bytes=48 * 1024 * 1024
        ),
        name="scatter_grads",
    )(grad_main, grad_low, gain_rows)


def gather_tokens_kernel(ctx_size, in_ref, out_ref, send, recv):
    dp_at, ctx_at, core, z_at, first, second, across = place()
    depth = ctx_size // 2
    sibling = (dp_at, ctx_at + 1 - 2 * core)
    z_peers = [(dp_at, 2 * lax.rem(z_at + i, depth) + core) for i in range(1, depth)]
    greet(z_peers + [sibling])
    out_ref[ctx_at] = in_ref[...]
    sent = []

    def push(ctx_from, targets):
        for target in targets:
            part = out_ref.at[ctx_from]
            one = remote(part, part, send.at[len(sent)], recv.at[ctx_from], target)
            one.start()
            sent.append(one)

    def arrive(ctx_from):
        part = out_ref.at[ctx_from]
        remote(part, part, send.at[0], recv.at[ctx_from], sibling).wait_recv()

    push(ctx_at, z_peers + [sibling])
    back = [lax.rem(z_at + depth - i, depth) for i in range(depth)]
    for z_from in back[1:]:
        arrive(2 * z_from + core)
        push(2 * z_from + core, [sibling])
    for z_from in back:
        arrive(2 * z_from + 1 - core)
    for one in sent:
        one.wait_send()


def gather_tokens(ctx_size, rows_in):
    count, width = rows_in.shape
    return pl.pallas_call(
        functools.partial(gather_tokens_kernel, ctx_size),
        out_shape=jax.ShapeDtypeStruct((ctx_size, count, width), BF),
        in_specs=vmem_specs(1),
        out_specs=vmem_specs(1)[0],
        scratch_shapes=[
            pltpu.SemaphoreType.DMA((ctx_size,)),
            pltpu.SemaphoreType.DMA((ctx_size,)),
        ],
        compiler_params=pltpu.CompilerParams(
            collective_id=2, has_side_effects=True, vmem_limit_bytes=48 * 1024 * 1024
        ),
        name="gather_tokens",
    )(rows_in)


def scatter_tokens_kernel(
    ctx_size, in_ref, out_ref, paired, along, send_c, recv_c, send_z, recv_z
):
    dp_at, ctx_at, core, z_at, first, second, across = place()
    depth = ctx_size // 2
    sibling = (dp_at, ctx_at + 1 - 2 * core)
    order = [lax.rem(z_at + i, depth) for i in range(1, depth + 1)]
    z_peers = [(dp_at, 2 * z_to + core) for z_to in order[:-1]]
    greet(z_peers + [sibling])
    sent = []
    for z_to in order:
        one = remote(
            in_ref.at[2 * z_to + 1 - core],
            paired.at[z_to],
            send_c.at[z_to],
            recv_c.at[z_to],
            sibling,
        )
        one.start()
        sent.append(one)
    for number, z_to in enumerate(order):
        part = paired.at[z_to]
        remote(part, part, send_c.at[z_to], recv_c.at[z_to], sibling).wait_recv()
        part[...] = (
            part[...].astype(F32) + in_ref[2 * z_to + core].astype(F32)
        ).astype(BF)
        if number < depth - 1:
            one = remote(
                part, along.at[z_at], send_z.at[z_to], recv_z.at[z_at], (dp_at, 2 * z_to + core)
            )
            one.start()
            sent.append(one)
    total = paired[z_at].astype(F32)
    for z_from in order[:-1]:
        part = along.at[z_from]
        remote(part, part, send_z.at[z_from], recv_z.at[z_from], sibling).wait_recv()
        total = total + part[...].astype(F32)
    out_ref[...] = total
    for one in sent:
        one.wait_send()


def scatter_tokens(ctx_size, parts):
    count, width = parts.shape[1:]
    depth = ctx_size // 2
    return pl.pallas_call(
        functools.partial(scatter_tokens_kernel, ctx_size),
        out_shape=jax.ShapeDtypeStruct((count, width), F32),
        in_specs=vmem_specs(1),
        out_specs=vmem_specs(1)[0],
        scratch_shapes=[
            pltpu.VMEM((depth, count, width), BF),
            pltpu.VMEM((depth, count, width), BF),
            pltpu.SemaphoreType.DMA((depth,)),
            pltpu.SemaphoreType.DMA((depth,)),
            pltpu.SemaphoreType.DMA((depth,)),
            pltpu.SemaphoreType.DMA((depth,)),
        ],
        compiler_params=pltpu.CompilerParams(
            collective_id=3, has_side_effects=True, vmem_limit_bytes=48 * 1024 * 1024
        ),
        name="scatter_tokens",
    )(parts)


def dot(left, right):
    return jnp.dot(left, right, preferred_element_type=F32)


def shuffle_matrix(shards):
    natural = lax.broadcasted_iota(jnp.int32, (D, D), 0)
    moved = lax.broadcasted_iota(jnp.int32, (D, D), 1)
    owner = natural // 18
    within = natural % 18
    wanted = jnp.where(within < MAIN, owner * MAIN + within, 512 + owner * 2 + within - MAIN)
    return jnp.where(wanted == moved, 1.0, 0.0).astype(BF)


def put_back(values, shuffle):
    upper = lax.reduce_precision(values, 8, 7)
    return against(upper.astype(BF), shuffle) + against((values - upper).astype(BF), shuffle)


def split_tail(w_query, w_key, w_value, w_output, w_gate, w_up):
    mats = [flat.reshape(18, -1) for flat in (w_query, w_key, w_output, w_value)]
    first_slab = jnp.concatenate(mats, axis=1)
    slabs = jnp.stack([first_slab, w_gate.reshape(18, FF), w_up.reshape(18, FF)])
    tail = slabs[:, MAIN:, :].reshape(3, 2, 2, PACK).transpose(0, 2, 1, 3).reshape(12, PACK)
    return (slabs[:, :MAIN, :], tail)


def fast_device(
    inputs, norm_gains, w_query, w_key, w_value, w_output, w_gate, w_up, w_down, cotangent
):
    ctx_size = lax.axis_size("ctx")
    shards = 4 * ctx_size
    micro = inputs.shape[0]
    row_count = inputs.shape[2]
    tokens = micro * row_count
    seq_length = row_count * ctx_size
    first_row = lax.axis_index("ctx") * row_count
    gain_width = D // ctx_size
    group_size = H // KV
    main, tail = split_tail(w_query, w_key, w_value, w_output, w_gate, w_up)
    gain_parts = []
    left = norm_gains
    for step in range(3):
        piece = lax.reduce_precision(left, 8, 7)
        gain_parts.append(piece)
        left = left - piece
    gain_rows = jnp.pad(
        jnp.stack(gain_parts), ((0, 1), (0, 0), (0, PACK // 2 - gain_width))
    ).reshape(4, PACK)
    tail = jnp.concatenate([tail, gain_rows.astype(BF)], axis=0)
    weights, down_mat, gain_blocks = gather_weights(
        ctx_size, main, w_down.reshape(48, D), tail
    )
    gain_blocks = gain_blocks.reshape(ctx_size, 16, 2, PACK // 2)[:, 12:15, :, :gain_width]
    gains = (
        jnp.sum(gain_blocks.astype(F32), axis=1).transpose(1, 0, 2).reshape(2, D)
    )
    query_mat = weights[0, :, 0:576]
    key_mat = weights[0, :, 576:768]
    output_mat = weights[0, :, 768:1344]
    value_mat = weights[0, :, 1344:1536]
    gate_mat = weights[1]
    up_mat = weights[2]
    shuffle = shuffle_matrix(shards)
    cosine, sine_table = rope_tables(first_row + jnp.arange(row_count))
    cosine = jnp.concatenate([cosine] * micro, axis=0)
    sine_table = jnp.concatenate([sine_table] * micro, axis=0)
    x_float = inputs.reshape(tokens, D).astype(F32)
    grad_out = cotangent.reshape(tokens, D)
    scale_one = rms_scale(x_float)
    normed_one = dot((x_float * scale_one * gains[0]).astype(BF), shuffle).astype(BF)
    queries = (
        rotate(dot(normed_one, query_mat), cosine, sine_table, H, 1.0) * score_scale
    ).astype(BF)
    key_rows = rotate(dot(normed_one, key_mat), cosine, sine_table, KV, 1.0).astype(BF)
    value_rows = dot(normed_one, value_mat).astype(BF)
    gathered = gather_tokens(ctx_size, jnp.concatenate([key_rows, value_rows], axis=1))
    gathered = (
        gathered.reshape(ctx_size, micro, row_count, 2, KV, HD)
        .transpose(3, 1, 4, 0, 2, 5)
        .reshape(2, micro, KV, seq_length, HD)
    )
    keys_all = gathered[0]
    values_all = gathered[1]

    def to_heads(values):
        return (
            values.reshape(micro, row_count, KV, group_size, HD)
            .transpose(0, 2, 3, 1, 4)
            .reshape(micro, KV, group_size * row_count, HD)
        )

    def from_heads(values):
        return (
            values.reshape(micro, KV, group_size, row_count, HD)
            .transpose(0, 3, 1, 2, 4)
            .reshape(tokens, H * HD)
        )

    grouped = to_heads(queries)
    scores = jnp.einsum("mkqd,mknd->mkqn", grouped, keys_all, preferred_element_type=F32)
    query_pos = first_row + jnp.arange(group_size * row_count) % row_count
    visible = jnp.arange(seq_length)[None, :] <= query_pos[:, None]
    masked = jnp.where(visible, scores, big_negative)
    weights_un = jnp.exp(masked - jnp.max(masked, axis=-1, keepdims=True))
    probs = weights_un / jnp.sum(weights_un, axis=-1, keepdims=True)
    probs_low = probs.astype(BF)
    mixed = jnp.einsum("mkqn,mknd->mkqd", probs_low, values_all, preferred_element_type=F32)
    attended = dot(from_heads(mixed).astype(BF), shuffle).astype(BF)
    residual = x_float + dot(attended, output_mat)
    scale_two = rms_scale(residual)
    normed_two = dot((residual * scale_two * gains[1]).astype(BF), shuffle).astype(BF)
    gate_pre = dot(normed_two, gate_mat)
    up_pre = dot(normed_two, up_mat)
    gate_sig = jax.nn.sigmoid(gate_pre)
    swish_val = gate_pre * gate_sig
    activated = (swish_val * up_pre).astype(BF)
    outcome = residual + dot(activated, down_mat)
    grad_act = against(grad_out, down_mat)
    grad_gate_pre = (grad_act * up_pre * gate_sig * (1.0 + gate_pre * (1.0 - gate_sig))).astype(BF)
    grad_up_pre = (grad_act * swish_val).astype(BF)
    grad_norm_two = put_back(
        against(grad_gate_pre, gate_mat) + against(grad_up_pre, up_mat), shuffle
    )
    gain_two = jnp.sum(grad_norm_two * residual * scale_two, axis=0)
    grad_residual = grad_out.astype(F32) + norm_back(grad_norm_two, residual, scale_two, gains[1])
    grad_branch = grad_residual.astype(BF)
    grad_attn = against(against(grad_branch, output_mat).astype(BF), shuffle).astype(BF)
    grad_grouped = to_heads(grad_attn)
    grad_probs = jnp.einsum(
        "mkqd,mknd->mkqn", grad_grouped, values_all, preferred_element_type=F32
    )
    delta = jnp.sum(grad_grouped.astype(F32) * mixed, axis=-1, keepdims=True)
    grad_scores = (probs * (grad_probs - delta)).astype(BF)
    grad_values = jnp.einsum(
        "mkqn,mkqd->mknd", probs_low, grad_grouped, preferred_element_type=F32
    )
    grad_keys = jnp.einsum("mkqn,mkqd->mknd", grad_scores, grouped, preferred_element_type=F32)
    grad_query = from_heads(
        jnp.einsum("mkqn,mknd->mkqd", grad_scores, keys_all, preferred_element_type=F32)
    )
    token_parts = (
        jnp.stack([grad_keys, grad_values])
        .astype(BF)
        .reshape(2, micro, KV, ctx_size, row_count, HD)
        .transpose(3, 1, 4, 0, 2, 5)
        .reshape(ctx_size, tokens, 2 * KV * HD)
    )
    summed = scatter_tokens(ctx_size, token_parts)
    grad_q_low = (rotate(grad_query, cosine, sine_table, H, -1.0) * score_scale).astype(BF)
    grad_k_low = rotate(summed[:, : KV * HD], cosine, sine_table, KV, -1.0).astype(BF)
    grad_v_low = summed[:, KV * HD :].astype(BF)
    grad_norm_one = put_back(
        against(grad_q_low, query_mat)
        + against(grad_k_low, key_mat)
        + against(grad_v_low, value_mat),
        shuffle,
    )
    gain_one = jnp.sum(grad_norm_one * x_float * scale_one, axis=0)
    grad_x = grad_residual + norm_back(grad_norm_one, x_float, scale_one, gains[0])
    grad_main = jnp.stack(
        [
            jnp.concatenate(
                [
                    across_rows(normed_one, grad_q_low),
                    across_rows(normed_one, grad_k_low),
                    across_rows(attended, grad_branch),
                    across_rows(normed_one, grad_v_low),
                ],
                axis=1,
            ).astype(BF),
            across_rows(normed_two, grad_gate_pre).astype(BF),
            across_rows(normed_two, grad_up_pre).astype(BF),
        ]
    )
    grad_low = across_rows(activated, grad_out).astype(BF)
    gain_local = jnp.stack([gain_one, gain_two]).reshape(2, ctx_size, gain_width)
    gain_pack = jnp.pad(
        gain_local.transpose(1, 0, 2), ((0, 0), (0, 0), (0, PACK // 2 - gain_width))
    ).reshape(ctx_size, 1, PACK)
    gain_pack = jnp.pad(gain_pack, ((0, 0), (12, 3), (0, 0))).reshape(ctx_size * 16, PACK)
    own_main, own_low, own_tail = scatter_grads(
        ctx_size, grad_main, grad_low, gain_pack.astype(BF)
    )
    tail_rows = own_tail[:12].reshape(3, 2, 2, PACK).transpose(0, 2, 1, 3).reshape(3, 2, FF)
    owned = jnp.concatenate([own_main, tail_rows], axis=1)
    gain_share = own_tail[12].reshape(2, PACK // 2)[:, :gain_width]
    shape_out = inputs.shape
    return (
        outcome.astype(BF).reshape(shape_out),
        grad_x.astype(BF).reshape(shape_out),
        gain_share,
        owned[0, :, 0:576].reshape(-1),
        owned[0, :, 576:768].reshape(-1),
        owned[0, :, 1344:1536].reshape(-1),
        owned[0, :, 768:1344].reshape(-1),
        owned[1].reshape(-1),
        owned[2].reshape(-1),
        own_low.reshape(-1),
    )


def solution(mesh):
    sizes = dict(mesh.shape)
    if sizes["dp"] != 4 or sizes["ctx"] % 2 or sizes["dp"] * sizes["ctx"] * 18 != D:
        return general_solution(mesh)
    tokens_spec = P(None, "dp", "ctx", None)
    flat_spec = P(("dp", "ctx"))
    return jax.shard_map(
        fast_device,
        mesh=mesh,
        in_specs=(tokens_spec, P(None, "ctx")) + (flat_spec,) * 7 + (tokens_spec,),
        out_specs=(tokens_spec, tokens_spec, P(None, "ctx")) + (flat_spec,) * 7,
        check_vma=False,
    )
```

```python
import functools
import jax
import jax.numpy as jnp
from jax import lax
from jax.experimental import pallas as pl
from jax.experimental.pallas import tpu as pltpu
from jax.sharding import PartitionSpec as P

D = 576
H = 9
KV = 3
HD = 64
FF = 1536


eps = 1e-05
rope_base = 10000.0
score_scale = 0.125
big_negative = -1e30


def rms_scale(values):
    return lax.rsqrt(jnp.mean(values * values, axis=-1, keepdims=True) + eps)


def norm_back(grad_out, values, row_scale, gain_row):
    weighted = grad_out * gain_row
    cubed = row_scale * row_scale * row_scale
    return row_scale * weighted - values * cubed * jnp.mean(
        weighted * values, axis=-1, keepdims=True
    )


def rope_tables(positions):
    half_size = HD // 2
    frequency = rope_base ** (-jnp.arange(half_size, dtype=jnp.float32) / half_size)
    angles = positions.astype(jnp.float32)[:, None] * frequency[None, :]
    return (jnp.cos(angles), jnp.sin(angles))


def rotate(values, cosine, sine_table, head_count, direction):
    row_count = values.shape[0]
    shaped = values.reshape(row_count, head_count, 2, HD // 2)
    first_half = shaped[:, :, 0, :]
    second_half = shaped[:, :, 1, :]
    cos_rows = cosine[:, None, :]
    sin_rows = direction * sine_table[:, None, :]
    turned = jnp.stack(
        [
            first_half * cos_rows - second_half * sin_rows,
            second_half * cos_rows + first_half * sin_rows,
        ],
        axis=2,
    )
    return turned.reshape(row_count, head_count * HD)


def across_rows(left_side, right_side):
    return lax.dot_general(
        left_side, right_side, (((0,), (0,)), ((), ())), preferred_element_type=jnp.float32
    )


def against(left_side, right_side):
    return lax.dot_general(
        left_side, right_side, (((1,), (1,)), ((), ())), preferred_element_type=jnp.float32
    )


def unpack(gathered, piece_sizes):
    mat_shapes = ((D, H * HD), (D, KV * HD), (D, KV * HD), (H * HD, D), (D, FF), (D, FF), (FF, D))
    matrices = []
    offset = 0
    for piece_len, mat_shape in zip(piece_sizes, mat_shapes):
        matrices.append(gathered[:, offset : offset + piece_len].reshape(mat_shape))
        offset = offset + piece_len
    return tuple(matrices)


def block_scores(queries, gathered_kv, block_index, key_block, first_row):
    row_count = queries.shape[0]
    key_rows = lax.dynamic_slice_in_dim(gathered_kv, block_index * key_block, key_block, 0)
    key_part = key_rows[:, : KV * HD].reshape(key_block, KV, HD)
    value_part = key_rows[:, KV * HD :].reshape(key_block, KV, HD)
    grouped = queries.reshape(row_count, KV, H // KV, HD)
    scores = jnp.einsum("qkgd,nkd->kgqn", grouped, key_part, preferred_element_type=jnp.float32)
    query_pos = first_row + jnp.arange(row_count)
    key_pos = block_index * key_block + jnp.arange(key_block)
    visible = key_pos[None, :] <= query_pos[:, None]
    return (scores, visible, key_part, value_part, grouped)


def attend(queries, gathered_kv, first_row, key_block, block_count):
    row_count = queries.shape[0]
    group_size = H // KV

    def running(block_index, state_pair):
        row_max, row_total = state_pair
        scores, visible, key_part, value_part, grouped = block_scores(
            queries, gathered_kv, block_index, key_block, first_row
        )
        masked = jnp.where(visible, scores, big_negative)
        new_max = jnp.maximum(row_max, jnp.max(masked, axis=-1))
        weights = jnp.where(visible, jnp.exp(masked - new_max[..., None]), 0.0)
        return (new_max, row_total * jnp.exp(row_max - new_max) + jnp.sum(weights, axis=-1))

    initial = (
        jnp.full((KV, group_size, row_count), big_negative, jnp.float32),
        jnp.zeros((KV, group_size, row_count), jnp.float32),
    )
    row_max, row_total = lax.fori_loop(0, block_count, running, initial)
    log_total = row_max + jnp.log(row_total)

    def weighted_sum(block_index, accum):
        scores, visible, key_part, value_part, grouped = block_scores(
            queries, gathered_kv, block_index, key_block, first_row
        )
        weights_low = jnp.where(visible, jnp.exp(scores - log_total[..., None]), 0.0).astype(
            jnp.bfloat16
        )
        return accum + jnp.einsum(
            "kgqn,nkd->qkgd", weights_low, value_part, preferred_element_type=jnp.float32
        )

    attn_mixed = lax.fori_loop(
        0, block_count, weighted_sum, jnp.zeros((row_count, KV, group_size, HD), jnp.float32)
    )
    return (attn_mixed.reshape(row_count, H * HD), log_total)


def attend_back(
    queries, gathered_kv, first_row, key_block, block_count, log_total, grad_grouped, delta
):
    row_count = queries.shape[0]
    group_size = H // KV

    def back_step(block_index, grad_query):
        scores, visible, key_part, value_part, grouped = block_scores(
            queries, gathered_kv, block_index, key_block, first_row
        )
        weights = jnp.where(visible, jnp.exp(scores - log_total[..., None]), 0.0)
        grad_weights = jnp.einsum(
            "qkgd,nkd->kgqn", grad_grouped, value_part, preferred_element_type=jnp.float32
        )
        grad_scores = (weights * (grad_weights - delta[..., None])).astype(jnp.bfloat16)
        return grad_query + jnp.einsum(
            "kgqn,nkd->qkgd", grad_scores, key_part, preferred_element_type=jnp.float32
        )

    grad_query = lax.fori_loop(
        0, block_count, back_step, jnp.zeros((row_count, KV, group_size, HD), jnp.float32)
    )
    return grad_query.reshape(row_count, H * HD)


def key_side(own_keys, own_values, key_first, stats, carry, pieces):
    query_piece, grad_piece = pieces
    lse_all, delta_all = stats
    piece_rows = query_piece.shape[0]
    block_rows = min(512, piece_rows)
    group_size = H // KV
    own_count = own_keys.shape[0]
    key_pos = key_first + jnp.arange(own_count, dtype=jnp.int32)

    def block_step(accums, block_index):
        grad_key, grad_value = accums
        row_start = block_index * block_rows
        query_block = lax.dynamic_slice_in_dim(query_piece, row_start, block_rows, 0).reshape(
            block_rows, KV, group_size, HD
        )
        grad_block = lax.dynamic_slice_in_dim(grad_piece, row_start, block_rows, 0).reshape(
            block_rows, KV, group_size, HD
        )
        lse_block = lax.dynamic_slice_in_dim(lse_all, row_start, block_rows, 1).reshape(
            KV, group_size, block_rows
        )
        delta_block = lax.dynamic_slice_in_dim(delta_all, row_start, block_rows, 1).reshape(
            KV, group_size, block_rows
        )
        scores = jnp.einsum(
            "qkgd,nkd->kgqn", query_block, own_keys, preferred_element_type=jnp.float32
        )
        query_pos = row_start + jnp.arange(block_rows, dtype=jnp.int32)
        visible = key_pos[None, :] <= query_pos[:, None]
        weights = jnp.where(visible, jnp.exp(scores - lse_block[..., None]), 0.0)
        grad_value = grad_value + jnp.einsum(
            "kgqn,qkgd->nkd",
            weights.astype(jnp.bfloat16),
            grad_block,
            preferred_element_type=jnp.float32,
        )
        grad_weights = jnp.einsum(
            "qkgd,nkd->kgqn", grad_block, own_values, preferred_element_type=jnp.float32
        )
        grad_scores = (weights * (grad_weights - delta_block[..., None])).astype(jnp.bfloat16)
        grad_key = grad_key + jnp.einsum(
            "kgqn,qkgd->nkd", grad_scores, query_block, preferred_element_type=jnp.float32
        )
        return ((grad_key, grad_value), None)

    outcome, ignored = lax.scan(
        block_step, carry, jnp.arange(piece_rows // block_rows, dtype=jnp.int32)
    )
    return outcome


def on_device(
    inputs, norm_gains, w_query, w_key, w_value, w_output, w_gate, w_up, w_down, cotangent
):
    ctx_size = lax.axis_size("ctx")
    device_count = lax.axis_size("dp") * ctx_size
    row_count = inputs.shape[2]
    seq_length = row_count * ctx_size
    first_row = lax.axis_index("ctx") * row_count
    key_block = min(512, seq_length)
    block_count = (first_row + row_count - 1) // key_block + 1
    group_size = H // KV
    cosine, sine_table = rope_tables(first_row + jnp.arange(row_count))
    weight_flats = (w_query, w_key, w_value, w_output, w_gate, w_up, w_down)
    piece_sizes = [flat_piece.shape[0] for flat_piece in weight_flats]
    packed = jnp.concatenate([flat_piece.reshape(1, -1) for flat_piece in weight_flats], axis=1)
    saved_rows = []
    out_rows = []
    grad_rows = []
    gain_terms = []
    for micro_batch in range(inputs.shape[0]):
        matrices = unpack(lax.all_gather(packed, ("dp", "ctx"), axis=0, tiled=True), piece_sizes)
        gain_rows = lax.all_gather(norm_gains, "ctx", axis=1, tiled=True)
        query_mat, key_mat, value_mat, output_mat, gate_mat, up_mat, down_mat = matrices
        x_float = inputs[micro_batch, 0].astype(jnp.float32)
        scale_one = rms_scale(x_float)
        normed_one = (x_float * scale_one * gain_rows[0]).astype(jnp.bfloat16)
        queries = (
            rotate(
                jnp.dot(normed_one, query_mat, preferred_element_type=jnp.float32),
                cosine,
                sine_table,
                H,
                1.0,
            )
            * score_scale
        ).astype(jnp.bfloat16)
        key_rows = rotate(
            jnp.dot(normed_one, key_mat, preferred_element_type=jnp.float32),
            cosine,
            sine_table,
            KV,
            1.0,
        ).astype(jnp.bfloat16)
        value_rows = jnp.dot(normed_one, value_mat, preferred_element_type=jnp.float32).astype(
            jnp.bfloat16
        )
        gathered_kv = lax.all_gather(
            jnp.concatenate([key_rows, value_rows], axis=1), "ctx", axis=0, tiled=True
        )
        attn_mixed, log_total = attend(queries, gathered_kv, first_row, key_block, block_count)
        attended = attn_mixed.astype(jnp.bfloat16)
        residual = x_float + jnp.dot(attended, output_mat, preferred_element_type=jnp.float32)
        scale_two = rms_scale(residual)
        normed_two = (residual * scale_two * gain_rows[1]).astype(jnp.bfloat16)
        gate_pre = jnp.dot(normed_two, gate_mat, preferred_element_type=jnp.float32)
        up_pre = jnp.dot(normed_two, up_mat, preferred_element_type=jnp.float32)
        gate_sig = jax.nn.sigmoid(gate_pre)
        swish_val = gate_pre * gate_sig
        activated = (swish_val * up_pre).astype(jnp.bfloat16)
        outcome = residual + jnp.dot(activated, down_mat, preferred_element_type=jnp.float32)
        out_rows.append(outcome.astype(jnp.bfloat16))
        query_back, key_back, value_back, output_back, gate_back, up_back, down_back = matrices
        grad_out = cotangent[micro_batch, 0]
        grad_act = against(grad_out, down_back)
        grad_gate_pre = (grad_act * up_pre * gate_sig * (1.0 + gate_pre * (1.0 - gate_sig))).astype(
            jnp.bfloat16
        )
        grad_up_pre = (grad_act * swish_val).astype(jnp.bfloat16)
        grad_norm_two = against(grad_gate_pre, gate_back) + against(grad_up_pre, up_back)
        gain_two = jnp.sum(grad_norm_two * residual * scale_two, axis=0)
        grad_residual = grad_out.astype(jnp.float32) + norm_back(
            grad_norm_two, residual, scale_two, gain_rows[1]
        )
        grad_branch = grad_residual.astype(jnp.bfloat16)
        grad_attn = against(grad_branch, output_back).astype(jnp.bfloat16)
        grad_grouped = grad_attn.reshape(row_count, KV, group_size, HD)
        product = (grad_attn.astype(jnp.float32) * attn_mixed).reshape(
            row_count, KV, group_size, HD
        )
        delta = jnp.transpose(jnp.sum(product, axis=-1), (1, 2, 0))
        grad_query = attend_back(
            queries, gathered_kv, first_row, key_block, block_count, log_total, grad_grouped, delta
        )
        stats = (
            lax.all_gather(log_total.reshape(H, row_count), "ctx", axis=1, tiled=True),
            lax.all_gather(delta.reshape(H, row_count), "ctx", axis=1, tiled=True),
        )
        own_keys = key_rows.reshape(row_count, KV, HD)
        own_values = value_rows.reshape(row_count, KV, HD)
        zero_rows = jnp.zeros((row_count, KV, HD), jnp.float32)
        grad_key_sum, grad_value_sum = key_side(
            own_keys,
            own_values,
            first_row,
            stats,
            (zero_rows, zero_rows),
            (
                lax.all_gather(queries, "ctx", axis=0, tiled=True),
                lax.all_gather(grad_attn, "ctx", axis=0, tiled=True),
            ),
        )
        grad_q_low = (rotate(grad_query, cosine, sine_table, H, -1.0) * score_scale).astype(
            jnp.bfloat16
        )
        grad_k_low = rotate(
            grad_key_sum.reshape(row_count, KV * HD), cosine, sine_table, KV, -1.0
        ).astype(jnp.bfloat16)
        grad_v_low = grad_value_sum.reshape(row_count, KV * HD).astype(jnp.bfloat16)
        grad_norm_one = (
            against(grad_q_low, query_back)
            + against(grad_k_low, key_back)
            + against(grad_v_low, value_back)
        )
        gain_one = jnp.sum(grad_norm_one * x_float * scale_one, axis=0)
        grad_x = grad_residual + norm_back(grad_norm_one, x_float, scale_one, gain_rows[0])
        grad_rows.append(grad_x.astype(jnp.bfloat16))
        gain_terms.append(jnp.stack([gain_one, gain_two], axis=0))
        saved_rows.append(
            (
                normed_one,
                grad_q_low,
                grad_k_low,
                grad_v_low,
                attended,
                grad_branch,
                normed_two,
                grad_gate_pre,
                grad_up_pre,
                activated,
                grad_out,
            )
        )
    joined = [
        jnp.concatenate([saved_set[member] for saved_set in saved_rows], axis=0)
        for member in range(11)
    ]
    local_grads = (
        across_rows(joined[0], joined[1]),
        across_rows(joined[0], joined[2]),
        across_rows(joined[0], joined[3]),
        across_rows(joined[4], joined[5]),
        across_rows(joined[6], joined[7]),
        across_rows(joined[6], joined[8]),
        across_rows(joined[9], joined[10]),
    )
    grad_table = jnp.concatenate(
        [grad_mat.reshape(device_count, -1) for grad_mat in local_grads], axis=1
    )
    owned = lax.psum_scatter(grad_table, ("dp", "ctx"), scatter_dimension=0, tiled=True)
    owned_parts = []
    offset = 0
    for piece_len in piece_sizes:
        owned_parts.append(owned[0, offset : offset + piece_len])
        offset = offset + piece_len
    gain_local = gain_terms[0]
    for extra_term in gain_terms[1:]:
        gain_local = gain_local + extra_term
    gain_total = lax.psum(gain_local, ("dp", "ctx"))
    gain_width = D // ctx_size
    gain_share = lax.dynamic_slice_in_dim(
        gain_total, lax.axis_index("ctx") * gain_width, gain_width, 1
    )
    return (
        jnp.stack(out_rows)[:, None],
        jnp.stack(grad_rows)[:, None],
        gain_share,
        owned_parts[0],
        owned_parts[1],
        owned_parts[2],
        owned_parts[3],
        owned_parts[4],
        owned_parts[5],
        owned_parts[6],
    )


def general_solution(mesh):
    placed = (
        P(None, "dp", "ctx", None),
        P(None, "ctx"),
        P(("dp", "ctx")),
        P(("dp", "ctx")),
        P(("dp", "ctx")),
        P(("dp", "ctx")),
        P(("dp", "ctx")),
        P(("dp", "ctx")),
        P(("dp", "ctx")),
        P(None, "dp", "ctx", None),
    )
    return jax.shard_map(
        on_device,
        mesh=mesh,
        in_specs=placed,
        out_specs=(
            P(None, "dp", "ctx", None),
            P(None, "dp", "ctx", None),
            P(None, "ctx"),
            P(("dp", "ctx")),
            P(("dp", "ctx")),
            P(("dp", "ctx")),
            P(("dp", "ctx")),
            P(("dp", "ctx")),
            P(("dp", "ctx")),
            P(("dp", "ctx")),
        ),
        check_vma=False,
    )


BF = jnp.bfloat16
F32 = jnp.float32
MESH = pl.DeviceIdType.MESH
MAIN = 16
PACK = 768


def place():
    dp_at = lax.axis_index("dp")
    ctx_at = lax.axis_index("ctx")
    core = lax.rem(ctx_at, 2)
    flip_one = dp_at + 1 - 2 * lax.rem(dp_at, 2)
    flip_two = lax.rem(dp_at + 2, 4)
    first = (1 - core) * flip_one + core * flip_two
    second = (1 - core) * flip_two + core * flip_one
    return (dp_at, ctx_at, core, ctx_at // 2, first, second, 3 - dp_at)


def greet(targets):
    barrier = pltpu.get_barrier_semaphore()
    for target in targets:
        pl.semaphore_signal(barrier, inc=1, device_id=target, device_id_type=MESH)
    pl.semaphore_wait(barrier, len(targets))


def rows(index, size):
    return pl.ds(pl.multiple_of(index * size, size), size)


def remote(src, dst, send, recv, target):
    return pltpu.make_async_remote_copy(
        src_ref=src, dst_ref=dst, send_sem=send, recv_sem=recv, device_id=target, device_id_type=MESH
    )


def tail_matrix(shards, transposed):
    width = shards * MAIN
    shape = (width, 384) if transposed else (384, width)
    out_at = lax.broadcasted_iota(jnp.int32, shape, 1 if transposed else 0)
    in_at = lax.broadcasted_iota(jnp.int32, shape, 0 if transposed else 1)
    wanted = (lax.rem(out_at, 64) // 2) * MAIN + (out_at // 64) * 2 + lax.rem(out_at, 2)
    return jnp.where(wanted == in_at, 1.0, 0.0).astype(BF)


def view(ref, index, size):
    if len(ref.shape) == 3:
        return ref.at[:, rows(index, size), :]
    return ref.at[rows(index, size), :]


def vmem_specs(count):
    return [pl.BlockSpec(memory_space=pltpu.VMEM)] * count


def comm_params(number):
    return pltpu.CompilerParams(
        collective_id=number, has_side_effects=True, vmem_limit_bytes=56 * 1024 * 1024
    )


class WeightGather:
    def __init__(self, ctx_size, refs, sizes, send, recv):
        self.ctx_size = ctx_size
        self.refs = refs
        self.sizes = sizes
        self.send = send
        self.recv = recv
        self.sent = []
        dp_at, ctx_at, core, z_at, first, second, across = place()
        self.at = (dp_at, first, second, across)
        self.core = core
        depth = ctx_size // 2
        self.me = dp_at * ctx_size + ctx_at
        self.sibling = (dp_at, ctx_at + 1 - 2 * core)
        self.to_first = (first, ctx_at)
        self.to_second = (second, ctx_at)
        self.z_peers = [(dp_at, 2 * lax.rem(z_at + i, depth) + core) for i in range(1, depth)]
        self.back = [lax.rem(z_at + depth - i, depth) for i in range(depth)]
        self.targets = self.z_peers + [self.to_first, self.to_second, self.sibling]

    def copies(self, shard, target, slot):
        return [
            remote(
                view(ref, shard, size),
                view(ref, shard, size),
                self.send.at[slot, k],
                self.recv.at[shard, k],
                target,
            )
            for k, (ref, size) in enumerate(zip(self.refs, self.sizes))
        ]

    def push(self, shard, targets):
        for target in targets:
            group = self.copies(shard, target, len(self.sent))
            for one in group:
                one.start()
            self.sent.append(group)

    def arrive(self, shard):
        for one in self.copies(shard, self.sibling, 0):
            one.wait_recv()

    def begin(self):
        self.push(self.me, self.targets)

    def pass_on(self, shard, targets):
        self.arrive(shard)
        self.push(shard, targets)

    def along_z(self):
        for z_from in self.back[1:]:
            shard = self.at[0] * self.ctx_size + 2 * z_from + self.core
            self.pass_on(shard, [self.to_first, self.to_second, self.sibling])

    def across_dp(self, z_from):
        shard = self.at[1] * self.ctx_size + 2 * z_from + self.core
        self.pass_on(shard, [self.to_second, self.sibling])
        shard = self.at[2] * self.ctx_size + 2 * z_from + self.core
        self.pass_on(shard, [self.sibling])

    def corner(self, z_from):
        self.pass_on(self.at[3] * self.ctx_size + 2 * z_from + self.core, [self.sibling])

    def finish(self):
        for dp_from in self.at:
            for z_from in self.back:
                self.arrive(dp_from * self.ctx_size + 2 * z_from + 1 - self.core)
        for group in self.sent:
            for one in group:
                one.wait_send()


def gather_first_kernel(ctx_size, w_ref, t_ref, ow_ref, ox_ref, og_ref, tg_ref, send, recv):
    shards = 4 * ctx_size
    plan = WeightGather(ctx_size, (ow_ref, tg_ref), (16, 16), send, recv)
    greet(plan.targets)
    ow_ref[rows(plan.me, 16), :] = w_ref[...]
    tg_ref[rows(plan.me, 16), :] = t_ref[...]
    plan.begin()
    plan.along_z()
    for z_from in plan.back:
        plan.across_dp(z_from)
    for z_from in plan.back:
        plan.corner(z_from)
    plan.finish()
    unpacked = jnp.dot(
        tail_matrix(shards, False), tg_ref[...], preferred_element_type=F32
    ).astype(BF)
    for part in range(6):
        piece = unpacked[64 * part : 64 * part + 64]
        columns = slice((part % 2) * PACK, (part % 2 + 1) * PACK)
        if part < 2:
            ow_ref[512:576, columns] = piece
        else:
            ox_ref[part // 2 - 1, :, columns] = piece
    og_ref[...] = tg_ref[0 : ctx_size * 16, :]


def gather_first(ctx_size, w_main, w_tail):
    shards = 4 * ctx_size
    return pl.pallas_call(
        functools.partial(gather_first_kernel, ctx_size),
        out_shape=(
            jax.ShapeDtypeStruct((D, FF), BF),
            jax.ShapeDtypeStruct((2, 64, FF), BF),
            jax.ShapeDtypeStruct((ctx_size * 16, PACK), BF),
        ),
        in_specs=vmem_specs(2),
        out_specs=tuple(vmem_specs(3)),
        scratch_shapes=[
            pltpu.VMEM((shards * 16, PACK), BF),
            pltpu.SemaphoreType.DMA((shards, 2)),
            pltpu.SemaphoreType.DMA((shards, 2)),
        ],
        compiler_params=comm_params(0),
        name="gather_first",
    )(w_main, w_tail)


def head_rows(ref, micro, group, row_count):
    return jnp.concatenate(
        [
            ref[micro * row_count : (micro + 1) * row_count, HD * h : HD * h + HD]
            for h in range(3 * group, 3 * group + 3)
        ],
        axis=0,
    )


def attend_forward_kernel(
    ctx_size,
    w_ref,
    d_ref,
    x_ref,
    q_ref,
    kv_ref,
    ow_ref,
    od_ref,
    kvg_ref,
    mixed_ref,
    lse_ref,
    send,
    recv,
    send_t,
    recv_t,
):
    plan = WeightGather(ctx_size, (ow_ref, od_ref), (16, 48), send, recv)
    ctx_at = lax.axis_index("ctx")
    tokens = q_ref.shape[0]
    row_count = tokens // 2
    seq_length = ctx_size * row_count
    first_row = ctx_at * row_count
    core = plan.core
    greet(plan.targets)
    kvg_ref[ctx_at] = kv_ref[...]
    sent = []

    def push(ctx_from, targets):
        for target in targets:
            part = kvg_ref.at[ctx_from]
            one = remote(part, part, send_t.at[len(sent)], recv_t.at[ctx_from], target)
            one.start()
            sent.append(one)

    def arrive(ctx_from):
        part = kvg_ref.at[ctx_from]
        remote(part, part, send_t.at[0], recv_t.at[ctx_from], plan.sibling).wait_recv()

    push(ctx_at, plan.z_peers + [plan.sibling])
    ow_ref[:, rows(plan.me, 16), :] = w_ref[...]
    od_ref[rows(plan.me, 48), :] = d_ref[...]
    plan.begin()
    ow_ref[:, 512:576, :] = x_ref[...]
    for z_from in plan.back[1:]:
        arrive(2 * z_from + core)
        push(2 * z_from + core, [plan.sibling])
    plan.along_z()
    for z_from in plan.back:
        arrive(2 * z_from + 1 - core)
    services = [functools.partial(plan.across_dp, z_from) for z_from in plan.back]
    shape = (3 * row_count, seq_length)
    query_pos = first_row + lax.rem(lax.broadcasted_iota(jnp.int32, shape, 0), row_count)
    visible = lax.broadcasted_iota(jnp.int32, shape, 1) <= query_pos
    lanes = lax.broadcasted_iota(jnp.int32, (row_count, 128), 1)
    for micro in range(2):
        spot = slice(micro * row_count, (micro + 1) * row_count)
        logs = jnp.zeros((row_count, 128), F32)
        for group in range(KV):
            queries = head_rows(q_ref, micro, group, row_count)
            keys = kvg_ref[:, spot, HD * group : HD * group + HD].reshape(seq_length, HD)
            low = KV * HD + HD * group
            values = kvg_ref[:, spot, low : low + HD].reshape(seq_length, HD)
            scores = jnp.where(visible, against(queries, keys), big_negative)
            top = jnp.max(scores, axis=-1, keepdims=True)
            raised = jnp.exp(scores - top)
            total = jnp.sum(raised, axis=-1, keepdims=True)
            probs_low = (raised * (1.0 / total)).astype(BF)
            mixed = jnp.dot(probs_low, values, preferred_element_type=F32)
            log_total = top + jnp.log(total)
            for member in range(3):
                h = 3 * group + member
                part = slice(member * row_count, (member + 1) * row_count)
                mixed_ref[spot, HD * h : HD * h + HD] = mixed[part]
                logs = jnp.where(lanes == h, log_total[part], logs)
            if services:
                services.pop(0)()
        lse_ref[spot, :] = logs
    for service in services:
        service()
    for z_from in plan.back:
        plan.corner(z_from)
    plan.finish()
    for one in sent:
        one.wait_send()


def attend_forward(ctx_size, w_main, w_low, w_extra, queries, kv_rows):
    shards = 4 * ctx_size
    tokens = queries.shape[0]
    return pl.pallas_call(
        functools.partial(attend_forward_kernel, ctx_size),
        out_shape=(
            jax.ShapeDtypeStruct((2, D, FF), BF),
            jax.ShapeDtypeStruct((FF, D), BF),
            jax.ShapeDtypeStruct((ctx_size,) + kv_rows.shape, BF),
            jax.ShapeDtypeStruct((tokens, H * HD), F32),
            jax.ShapeDtypeStruct((tokens, 128), F32),
        ),
        in_specs=vmem_specs(5),
        out_specs=tuple(vmem_specs(5)),
        scratch_shapes=[
            pltpu.SemaphoreType.DMA((shards, 2)),
            pltpu.SemaphoreType.DMA((shards, 2)),
            pltpu.SemaphoreType.DMA((ctx_size,)),
            pltpu.SemaphoreType.DMA((ctx_size,)),
        ],
        compiler_params=comm_params(1),
        name="attend_forward",
    )(w_main, w_low, w_extra, queries, kv_rows)


class GradScatter:
    def __init__(self, ctx_size, own, sizes, slots, sems):
        self.own = own
        self.sizes = sizes
        count = len(own)
        self.paired, self.via, self.from_first, self.from_second, self.along = [
            slots[k * count : (k + 1) * count] for k in range(5)
        ]
        self.send_c, self.recv_c, self.send_d, self.recv_d, self.send_z, self.recv_z = sems
        self.ctx_size = ctx_size
        self.depth = ctx_size // 2
        dp_at, ctx_at, core, z_at, first, second, across = place()
        self.at = (dp_at, first, second, across)
        self.core = core
        self.z_at = z_at
        self.sibling = (dp_at, ctx_at + 1 - 2 * core)
        self.to_first = (first, ctx_at)
        self.to_second = (second, ctx_at)
        self.order = [lax.rem(z_at + i, self.depth) for i in range(1, self.depth + 1)]
        self.z_peers = [(dp_at, 2 * z_to + core) for z_to in self.order[:-1]]
        self.targets = self.z_peers + [self.to_first, self.to_second, self.sibling]
        self.sent = []

    def views(self, refs, index):
        return [view(ref, index, size) for ref, size in zip(refs, self.sizes)]

    def ship(self, src, dst, send, recv, target):
        group = [
            remote(src[k], dst[k], send.at[k], recv.at[k], target) for k in range(len(src))
        ]
        for one in group:
            one.start()
        self.sent.append(group)

    def arrive(self, dst, recv):
        for k in range(len(dst)):
            remote(dst[k], dst[k], recv.at[k], recv.at[k], self.sibling).wait_recv()

    def add(self, dst, terms):
        for k in range(len(dst)):
            total = dst[k][...].astype(F32)
            for term in terms:
                total = total + term[k][...].astype(F32)
            dst[k][...] = total.astype(BF)

    def begin(self):
        dp_at, first, second, across = self.at
        for z_to in self.order:
            for dp_to in (across, second, first, dp_at):
                shard = dp_to * self.ctx_size + 2 * z_to + 1 - self.core
                slot = dp_to * self.depth + z_to
                self.ship(
                    self.views(self.own, shard),
                    self.views(self.paired, slot),
                    self.send_c.at[slot],
                    self.recv_c.at[slot],
                    self.sibling,
                )

    def pair_up(self, dp_to, z_to):
        slot = dp_to * self.depth + z_to
        partial = self.views(self.paired, slot)
        self.arrive(partial, self.recv_c.at[slot])
        self.add(
            partial, [self.views(self.own, dp_to * self.ctx_size + 2 * z_to + self.core)]
        )
        return partial

    def leave(self, partial, slots, kind, z_to, target):
        self.ship(
            partial,
            self.views(slots, z_to),
            self.send_d.at[kind, z_to],
            self.recv_d.at[kind, z_to],
            target,
        )

    def pairs(self, z_to):
        dp_at, first, second, across = self.at
        self.leave(self.pair_up(across, z_to), self.via, 0, z_to, self.to_second)
        self.leave(self.pair_up(second, z_to), self.from_second, 1, z_to, self.to_second)
        self.pair_up(first, z_to)
        self.pair_up(dp_at, z_to)

    def relay(self, z_to):
        partial = self.views(self.paired, self.at[1] * self.depth + z_to)
        came = self.views(self.via, z_to)
        self.arrive(came, self.recv_d.at[0, z_to])
        self.add(partial, [came])
        self.leave(partial, self.from_first, 2, z_to, self.to_first)

    def gathered(self, number):
        z_to = self.order[number]
        partial = self.views(self.paired, self.at[0] * self.depth + z_to)
        ahead = self.views(self.from_second, z_to)
        aside = self.views(self.from_first, z_to)
        self.arrive(ahead, self.recv_d.at[1, z_to])
        self.arrive(aside, self.recv_d.at[2, z_to])
        self.add(partial, [ahead, aside])
        if number < self.depth - 1:
            self.ship(
                partial,
                self.views(self.along, self.z_at),
                self.send_z.at[z_to],
                self.recv_z.at[self.z_at],
                (self.at[0], 2 * z_to + self.core),
            )

    def finish(self, outs):
        for z_from in self.order[:-1]:
            self.arrive(self.views(self.along, z_from), self.recv_z.at[z_from])
        mine = self.views(self.paired, self.at[0] * self.depth + self.z_at)
        others = [self.views(self.along, z_from) for z_from in self.order[:-1]]
        for k, out in enumerate(outs):
            total = mine[k][...].astype(F32)
            for other in others:
                total = total + other[k][...].astype(F32)
            out[...] = total
        for group in self.sent:
            for one in group:
                one.wait_send()


def scatter_scratch(ctx_size, shapes):
    depth = ctx_size // 2
    slots = []
    for count in (4 * depth, depth, depth, depth, depth):
        for shape in shapes:
            slots.append(pltpu.VMEM(shape[:-2] + (count * shape[-2], shape[-1]), BF))
    kinds = len(shapes)
    pairs = [(4 * depth, kinds), (3, depth, kinds), (depth, kinds)]
    return slots + [pltpu.SemaphoreType.DMA(pair) for pair in pairs for twice in range(2)]


def attend_backward_kernel(
    ctx_size,
    gw_ref,
    gd_ref,
    q_ref,
    kvg_ref,
    ga_ref,
    mixed_ref,
    lse_ref,
    ow_ref,
    od_ref,
    dq_ref,
    dkv_ref,
    parts_ref,
    paired_t,
    along_t,
    send_c,
    recv_c,
    send_z,
    recv_z,
    *scratch
):
    plan = GradScatter(ctx_size, (gw_ref, gd_ref), (16, 48), scratch[:10], scratch[10:])
    ctx_at = lax.axis_index("ctx")
    tokens = q_ref.shape[0]
    row_count = tokens // 2
    seq_length = ctx_size * row_count
    first_row = ctx_at * row_count
    core = plan.core
    greet(plan.targets)
    plan.begin()
    services = [functools.partial(plan.pairs, z_to) for z_to in plan.order]
    services = services + [functools.partial(plan.relay, z_to) for z_to in plan.order]
    shape = (seq_length, 3 * row_count)
    query_pos = first_row + lax.rem(lax.broadcasted_iota(jnp.int32, shape, 1), row_count)
    visible = lax.broadcasted_iota(jnp.int32, shape, 0) <= query_pos
    lanes = lax.broadcasted_iota(jnp.int32, (row_count, 128), 1)
    for micro in range(2):
        spot = slice(micro * row_count, (micro + 1) * row_count)
        deltas = jnp.zeros((row_count, 128), F32)
        for h in range(H):
            columns = slice(HD * h, HD * h + HD)
            product = ga_ref[spot, columns].astype(F32) * mixed_ref[spot, columns]
            deltas = jnp.where(lanes == h, jnp.sum(product, axis=-1, keepdims=True), deltas)
        deltas = deltas.T
        logs = lse_ref[spot, :].T
        for group in range(KV):
            queries = head_rows(q_ref, micro, group, row_count)
            grads = head_rows(ga_ref, micro, group, row_count)
            low = KV * HD + HD * group
            keys = kvg_ref[:, spot, HD * group : HD * group + HD].reshape(seq_length, HD)
            values = kvg_ref[:, spot, low : low + HD].reshape(seq_length, HD)
            log_row = jnp.concatenate(
                [logs[h : h + 1] for h in range(3 * group, 3 * group + 3)], axis=1
            )
            delta_row = jnp.concatenate(
                [deltas[h : h + 1] for h in range(3 * group, 3 * group + 3)], axis=1
            )
            scores = jnp.where(visible, against(keys, queries), big_negative)
            probs = jnp.exp(scores - log_row)
            grad_value = jnp.dot(probs.astype(BF), grads, preferred_element_type=F32)
            grad_scores = (probs * (against(values, grads) - delta_row)).astype(BF)
            grad_key = jnp.dot(grad_scores, queries, preferred_element_type=F32)
            grad_query = across_rows(keys, grad_scores).T
            parts_ref[:, spot, HD * group : HD * group + HD] = grad_key.astype(BF).reshape(
                ctx_size, row_count, HD
            )
            parts_ref[:, spot, low : low + HD] = grad_value.astype(BF).reshape(
                ctx_size, row_count, HD
            )
            for member in range(3):
                h = 3 * group + member
                dq_ref[spot, HD * h : HD * h + HD] = grad_query[
                    member * row_count : (member + 1) * row_count
                ]
            if services:
                services.pop(0)()
    sent = []
    for z_to in plan.order:
        one = remote(
            parts_ref.at[2 * z_to + 1 - core],
            paired_t.at[z_to],
            send_c.at[z_to],
            recv_c.at[z_to],
            plan.sibling,
        )
        one.start()
        sent.append(one)
    for service in services:
        service()
    for number, z_to in enumerate(plan.order):
        part = paired_t.at[z_to]
        remote(part, part, send_c.at[z_to], recv_c.at[z_to], plan.sibling).wait_recv()
        part[...] = (
            part[...].astype(F32) + parts_ref[2 * z_to + core].astype(F32)
        ).astype(BF)
        if number < plan.depth - 1:
            one = remote(
                part,
                along_t.at[plan.z_at],
                send_z.at[z_to],
                recv_z.at[plan.z_at],
                (plan.at[0], 2 * z_to + core),
            )
            one.start()
            sent.append(one)
    for number in range(plan.depth):
        plan.gathered(number)
    total = paired_t[plan.z_at].astype(F32)
    for z_from in plan.order[:-1]:
        part = along_t.at[z_from]
        remote(part, part, send_z.at[z_from], recv_z.at[z_from], plan.sibling).wait_recv()
        total = total + part[...].astype(F32)
    dkv_ref[...] = total
    plan.finish((ow_ref, od_ref))
    for one in sent:
        one.wait_send()


def attend_backward(ctx_size, grad_main, grad_low, queries, kvg, grad_attn, mixed, lse):
    depth = ctx_size // 2
    tokens, width = kvg.shape[1:]
    return pl.pallas_call(
        functools.partial(attend_backward_kernel, ctx_size),
        out_shape=(
            jax.ShapeDtypeStruct((2, 16, FF), F32),
            jax.ShapeDtypeStruct((48, D), F32),
            jax.ShapeDtypeStruct((tokens, H * HD), F32),
            jax.ShapeDtypeStruct((tokens, width), F32),
        ),
        in_specs=vmem_specs(7),
        out_specs=tuple(vmem_specs(4)),
        scratch_shapes=[
            pltpu.VMEM((ctx_size, tokens, width), BF),
            pltpu.VMEM((depth, tokens, width), BF),
            pltpu.VMEM((depth, tokens, width), BF),
        ]
        + [pltpu.SemaphoreType.DMA((depth,))] * 4
        + scatter_scratch(ctx_size, ((2, 16, FF), (48, D))),
        compiler_params=comm_params(2),
        name="attend_backward",
    )(grad_main, grad_low, queries, kvg, grad_attn, mixed, lse)


def scatter_last_kernel(ctx_size, gw_ref, ge_ref, gx_ref, ow_ref, ot_ref, tail, *scratch):
    plan = GradScatter(ctx_size, (gw_ref, tail), (16, 16), scratch[:10], scratch[10:])
    greet(plan.targets)
    pieces = []
    for part in range(6):
        columns = slice((part % 2) * PACK, (part % 2 + 1) * PACK)
        if part < 2:
            pieces.append(gw_ref[512:576, columns])
        else:
            pieces.append(ge_ref[part // 2 - 1, :, columns])
    stacked = jnp.concatenate(pieces, axis=0)
    spread = jnp.dot(tail_matrix(4 * ctx_size, True), stacked, preferred_element_type=F32)
    for block in range(4):
        part = slice(block * ctx_size * 16, (block + 1) * ctx_size * 16)
        tail[part, :] = (spread[part] + gx_ref[...].astype(F32)).astype(BF)
    plan.begin()
    for z_to in plan.order:
        plan.pairs(z_to)
    for z_to in plan.order:
        plan.relay(z_to)
    for number in range(plan.depth):
        plan.gathered(number)
    plan.finish((ow_ref, ot_ref))


def scatter_last(ctx_size, grad_main, grad_extra, gain_rows):
    return pl.pallas_call(
        functools.partial(scatter_last_kernel, ctx_size),
        out_shape=(
            jax.ShapeDtypeStruct((16, FF), F32),
            jax.ShapeDtypeStruct((16, PACK), F32),
        ),
        in_specs=vmem_specs(3),
        out_specs=tuple(vmem_specs(2)),
        scratch_shapes=[pltpu.VMEM((4 * ctx_size * 16, PACK), BF)]
        + scatter_scratch(ctx_size, ((16, FF), (16, PACK))),
        compiler_params=comm_params(3),
        name="scatter_last",
    )(grad_main, grad_extra, gain_rows)


def dot(left, right):
    return jnp.dot(left, right, preferred_element_type=F32)


def shuffle_matrix(shards):
    natural = lax.broadcasted_iota(jnp.int32, (D, D), 0)
    moved = lax.broadcasted_iota(jnp.int32, (D, D), 1)
    owner = natural // 18
    within = natural % 18
    wanted = jnp.where(within < MAIN, owner * MAIN + within, 512 + owner * 2 + within - MAIN)
    return jnp.where(wanted == moved, 1.0, 0.0).astype(BF)


def put_back(values, shuffle):
    upper = lax.reduce_precision(values, 8, 7)
    return against(upper.astype(BF), shuffle) + against((values - upper).astype(BF), shuffle)


def split_tail(w_query, w_key, w_value, w_output, w_gate, w_up):
    mats = [flat.reshape(18, -1) for flat in (w_query, w_key, w_output, w_value)]
    first_slab = jnp.concatenate(mats, axis=1)
    slabs = jnp.stack([first_slab, w_gate.reshape(18, FF), w_up.reshape(18, FF)])
    tail = slabs[:, MAIN:, :].reshape(3, 2, 2, PACK).transpose(0, 2, 1, 3).reshape(12, PACK)
    return (slabs[:, :MAIN, :], tail)


def fast_device(
    inputs, norm_gains, w_query, w_key, w_value, w_output, w_gate, w_up, w_down, cotangent
):
    ctx_size = lax.axis_size("ctx")
    shards = 4 * ctx_size
    micro = inputs.shape[0]
    row_count = inputs.shape[2]
    tokens = micro * row_count
    first_row = lax.axis_index("ctx") * row_count
    gain_width = D // ctx_size
    main, tail = split_tail(w_query, w_key, w_value, w_output, w_gate, w_up)
    gain_parts = []
    left = norm_gains
    for step in range(3):
        piece = lax.reduce_precision(left, 8, 7)
        gain_parts.append(piece)
        left = left - piece
    gain_rows = jnp.pad(
        jnp.stack(gain_parts), ((0, 1), (0, 0), (0, PACK // 2 - gain_width))
    ).reshape(4, PACK)
    tail = jnp.concatenate([tail, gain_rows.astype(BF)], axis=0)
    attn_mats, tail_rows, gain_blocks = gather_first(ctx_size, main[0], tail)
    gain_blocks = gain_blocks.reshape(ctx_size, 16, 2, PACK // 2)[:, 12:15, :, :gain_width]
    gains = (
        jnp.sum(gain_blocks.astype(F32), axis=1).transpose(1, 0, 2).reshape(2, D)
    )
    query_mat = attn_mats[:, 0:576]
    key_mat = attn_mats[:, 576:768]
    output_mat = attn_mats[:, 768:1344]
    value_mat = attn_mats[:, 1344:1536]
    shuffle = shuffle_matrix(shards)
    cosine, sine_table = rope_tables(first_row + jnp.arange(row_count))
    cosine = jnp.concatenate([cosine] * micro, axis=0)
    sine_table = jnp.concatenate([sine_table] * micro, axis=0)
    x_float = inputs.reshape(tokens, D).astype(F32)
    grad_out = cotangent.reshape(tokens, D)
    scale_one = rms_scale(x_float)
    normed_one = dot((x_float * scale_one * gains[0]).astype(BF), shuffle).astype(BF)
    queries = (
        rotate(dot(normed_one, query_mat), cosine, sine_table, H, 1.0) * score_scale
    ).astype(BF)
    key_rows = rotate(dot(normed_one, key_mat), cosine, sine_table, KV, 1.0).astype(BF)
    value_rows = dot(normed_one, value_mat).astype(BF)
    ffn_mats, down_mat, gathered, mixed, log_total = attend_forward(
        ctx_size,
        main[1:],
        w_down.reshape(48, D),
        tail_rows,
        queries,
        jnp.concatenate([key_rows, value_rows], axis=1),
    )
    gate_mat = ffn_mats[0]
    up_mat = ffn_mats[1]
    attended = dot(mixed.astype(BF), shuffle).astype(BF)
    residual = x_float + dot(attended, output_mat)
    scale_two = rms_scale(residual)
    normed_two = dot((residual * scale_two * gains[1]).astype(BF), shuffle).astype(BF)
    gate_pre = dot(normed_two, gate_mat)
    up_pre = dot(normed_two, up_mat)
    gate_sig = jax.nn.sigmoid(gate_pre)
    swish_val = gate_pre * gate_sig
    activated = (swish_val * up_pre).astype(BF)
    outcome = residual + dot(activated, down_mat)
    grad_act = against(grad_out, down_mat)
    grad_gate_pre = (grad_act * up_pre * gate_sig * (1.0 + gate_pre * (1.0 - gate_sig))).astype(BF)
    grad_up_pre = (grad_act * swish_val).astype(BF)
    grad_norm_two = put_back(
        against(grad_gate_pre, gate_mat) + against(grad_up_pre, up_mat), shuffle
    )
    gain_two = jnp.sum(grad_norm_two * residual * scale_two, axis=0)
    grad_residual = grad_out.astype(F32) + norm_back(grad_norm_two, residual, scale_two, gains[1])
    grad_branch = grad_residual.astype(BF)
    grad_attn = against(against(grad_branch, output_mat).astype(BF), shuffle).astype(BF)
    grad_ffn = jnp.stack(
        [across_rows(normed_two, grad_gate_pre), across_rows(normed_two, grad_up_pre)]
    ).astype(BF)
    grad_low = across_rows(activated, grad_out).astype(BF)
    own_ffn, own_low, grad_query, summed = attend_backward(
        ctx_size, grad_ffn, grad_low, queries, gathered, grad_attn, mixed, log_total
    )
    grad_q_low = (rotate(grad_query, cosine, sine_table, H, -1.0) * score_scale).astype(BF)
    grad_k_low = rotate(summed[:, : KV * HD], cosine, sine_table, KV, -1.0).astype(BF)
    grad_v_low = summed[:, KV * HD :].astype(BF)
    grad_norm_one = put_back(
        against(grad_q_low, query_mat)
        + against(grad_k_low, key_mat)
        + against(grad_v_low, value_mat),
        shuffle,
    )
    gain_one = jnp.sum(grad_norm_one * x_float * scale_one, axis=0)
    grad_x = grad_residual + norm_back(grad_norm_one, x_float, scale_one, gains[0])
    grad_first = jnp.concatenate(
        [
            across_rows(normed_one, grad_q_low),
            across_rows(normed_one, grad_k_low),
            across_rows(attended, grad_branch),
            across_rows(normed_one, grad_v_low),
        ],
        axis=1,
    ).astype(BF)
    gain_local = jnp.stack([gain_one, gain_two]).reshape(2, ctx_size, gain_width)
    gain_pack = jnp.pad(
        gain_local.transpose(1, 0, 2), ((0, 0), (0, 0), (0, PACK // 2 - gain_width))
    ).reshape(ctx_size, 1, PACK)
    gain_pack = jnp.pad(gain_pack, ((0, 0), (12, 3), (0, 0))).reshape(ctx_size * 16, PACK)
    own_first, own_tail = scatter_last(
        ctx_size, grad_first, grad_ffn[:, 512:576], gain_pack.astype(BF)
    )
    own_main = jnp.concatenate([own_first[None], own_ffn], axis=0)
    tail_rows = own_tail[:12].reshape(3, 2, 2, PACK).transpose(0, 2, 1, 3).reshape(3, 2, FF)
    owned = jnp.concatenate([own_main, tail_rows], axis=1)
    gain_share = own_tail[12].reshape(2, PACK // 2)[:, :gain_width]
    shape_out = inputs.shape
    return (
        outcome.astype(BF).reshape(shape_out),
        grad_x.astype(BF).reshape(shape_out),
        gain_share,
        owned[0, :, 0:576].reshape(-1),
        owned[0, :, 576:768].reshape(-1),
        owned[0, :, 1344:1536].reshape(-1),
        owned[0, :, 768:1344].reshape(-1),
        owned[1].reshape(-1),
        owned[2].reshape(-1),
        own_low.reshape(-1),
    )


def solution(mesh):
    sizes = dict(mesh.shape)
    if sizes["dp"] != 4 or sizes["ctx"] % 2 or sizes["dp"] * sizes["ctx"] * 18 != D:
        return general_solution(mesh)
    tokens_spec = P(None, "dp", "ctx", None)
    flat_spec = P(("dp", "ctx"))
    return jax.shard_map(
        fast_device,
        mesh=mesh,
        in_specs=(tokens_spec, P(None, "ctx")) + (flat_spec,) * 7 + (tokens_spec,),
        out_specs=(tokens_spec, tokens_spec, P(None, "ctx")) + (flat_spec,) * 7,
        check_vma=False,
    )
```

```python
import functools
import jax
import jax.numpy as jnp
from jax import lax
from jax.experimental import pallas as pl
from jax.experimental.pallas import tpu as pltpu
from jax.sharding import PartitionSpec as P

D = 576
H = 9
KV = 3
HD = 64
FF = 1536


eps = 1e-05
rope_base = 10000.0
score_scale = 0.125
big_negative = -1e30


def rms_scale(values):
    return lax.rsqrt(jnp.mean(values * values, axis=-1, keepdims=True) + eps)


def norm_back(grad_out, values, row_scale, gain_row):
    weighted = grad_out * gain_row
    cubed = row_scale * row_scale * row_scale
    return row_scale * weighted - values * cubed * jnp.mean(
        weighted * values, axis=-1, keepdims=True
    )


def rope_tables(positions):
    half_size = HD // 2
    frequency = rope_base ** (-jnp.arange(half_size, dtype=jnp.float32) / half_size)
    angles = positions.astype(jnp.float32)[:, None] * frequency[None, :]
    return (jnp.cos(angles), jnp.sin(angles))


def rotate(values, cosine, sine_table, head_count, direction):
    row_count = values.shape[0]
    shaped = values.reshape(row_count, head_count, 2, HD // 2)
    first_half = shaped[:, :, 0, :]
    second_half = shaped[:, :, 1, :]
    cos_rows = cosine[:, None, :]
    sin_rows = direction * sine_table[:, None, :]
    turned = jnp.stack(
        [
            first_half * cos_rows - second_half * sin_rows,
            second_half * cos_rows + first_half * sin_rows,
        ],
        axis=2,
    )
    return turned.reshape(row_count, head_count * HD)


def across_rows(left_side, right_side):
    return lax.dot_general(
        left_side, right_side, (((0,), (0,)), ((), ())), preferred_element_type=jnp.float32
    )


def against(left_side, right_side):
    return lax.dot_general(
        left_side, right_side, (((1,), (1,)), ((), ())), preferred_element_type=jnp.float32
    )


def unpack(gathered, piece_sizes):
    mat_shapes = ((D, H * HD), (D, KV * HD), (D, KV * HD), (H * HD, D), (D, FF), (D, FF), (FF, D))
    matrices = []
    offset = 0
    for piece_len, mat_shape in zip(piece_sizes, mat_shapes):
        matrices.append(gathered[:, offset : offset + piece_len].reshape(mat_shape))
        offset = offset + piece_len
    return tuple(matrices)


def block_scores(queries, gathered_kv, block_index, key_block, first_row):
    row_count = queries.shape[0]
    key_rows = lax.dynamic_slice_in_dim(gathered_kv, block_index * key_block, key_block, 0)
    key_part = key_rows[:, : KV * HD].reshape(key_block, KV, HD)
    value_part = key_rows[:, KV * HD :].reshape(key_block, KV, HD)
    grouped = queries.reshape(row_count, KV, H // KV, HD)
    scores = jnp.einsum("qkgd,nkd->kgqn", grouped, key_part, preferred_element_type=jnp.float32)
    query_pos = first_row + jnp.arange(row_count)
    key_pos = block_index * key_block + jnp.arange(key_block)
    visible = key_pos[None, :] <= query_pos[:, None]
    return (scores, visible, key_part, value_part, grouped)


def attend(queries, gathered_kv, first_row, key_block, block_count):
    row_count = queries.shape[0]
    group_size = H // KV

    def running(block_index, state_pair):
        row_max, row_total = state_pair
        scores, visible, key_part, value_part, grouped = block_scores(
            queries, gathered_kv, block_index, key_block, first_row
        )
        masked = jnp.where(visible, scores, big_negative)
        new_max = jnp.maximum(row_max, jnp.max(masked, axis=-1))
        weights = jnp.where(visible, jnp.exp(masked - new_max[..., None]), 0.0)
        return (new_max, row_total * jnp.exp(row_max - new_max) + jnp.sum(weights, axis=-1))

    initial = (
        jnp.full((KV, group_size, row_count), big_negative, jnp.float32),
        jnp.zeros((KV, group_size, row_count), jnp.float32),
    )
    row_max, row_total = lax.fori_loop(0, block_count, running, initial)
    log_total = row_max + jnp.log(row_total)

    def weighted_sum(block_index, accum):
        scores, visible, key_part, value_part, grouped = block_scores(
            queries, gathered_kv, block_index, key_block, first_row
        )
        weights_low = jnp.where(visible, jnp.exp(scores - log_total[..., None]), 0.0).astype(
            jnp.bfloat16
        )
        return accum + jnp.einsum(
            "kgqn,nkd->qkgd", weights_low, value_part, preferred_element_type=jnp.float32
        )

    attn_mixed = lax.fori_loop(
        0, block_count, weighted_sum, jnp.zeros((row_count, KV, group_size, HD), jnp.float32)
    )
    return (attn_mixed.reshape(row_count, H * HD), log_total)


def attend_back(
    queries, gathered_kv, first_row, key_block, block_count, log_total, grad_grouped, delta
):
    row_count = queries.shape[0]
    group_size = H // KV

    def back_step(block_index, grad_query):
        scores, visible, key_part, value_part, grouped = block_scores(
            queries, gathered_kv, block_index, key_block, first_row
        )
        weights = jnp.where(visible, jnp.exp(scores - log_total[..., None]), 0.0)
        grad_weights = jnp.einsum(
            "qkgd,nkd->kgqn", grad_grouped, value_part, preferred_element_type=jnp.float32
        )
        grad_scores = (weights * (grad_weights - delta[..., None])).astype(jnp.bfloat16)
        return grad_query + jnp.einsum(
            "kgqn,nkd->qkgd", grad_scores, key_part, preferred_element_type=jnp.float32
        )

    grad_query = lax.fori_loop(
        0, block_count, back_step, jnp.zeros((row_count, KV, group_size, HD), jnp.float32)
    )
    return grad_query.reshape(row_count, H * HD)


def key_side(own_keys, own_values, key_first, stats, carry, pieces):
    query_piece, grad_piece = pieces
    lse_all, delta_all = stats
    piece_rows = query_piece.shape[0]
    block_rows = min(512, piece_rows)
    group_size = H // KV
    own_count = own_keys.shape[0]
    key_pos = key_first + jnp.arange(own_count, dtype=jnp.int32)

    def block_step(accums, block_index):
        grad_key, grad_value = accums
        row_start = block_index * block_rows
        query_block = lax.dynamic_slice_in_dim(query_piece, row_start, block_rows, 0).reshape(
            block_rows, KV, group_size, HD
        )
        grad_block = lax.dynamic_slice_in_dim(grad_piece, row_start, block_rows, 0).reshape(
            block_rows, KV, group_size, HD
        )
        lse_block = lax.dynamic_slice_in_dim(lse_all, row_start, block_rows, 1).reshape(
            KV, group_size, block_rows
        )
        delta_block = lax.dynamic_slice_in_dim(delta_all, row_start, block_rows, 1).reshape(
            KV, group_size, block_rows
        )
        scores = jnp.einsum(
            "qkgd,nkd->kgqn", query_block, own_keys, preferred_element_type=jnp.float32
        )
        query_pos = row_start + jnp.arange(block_rows, dtype=jnp.int32)
        visible = key_pos[None, :] <= query_pos[:, None]
        weights = jnp.where(visible, jnp.exp(scores - lse_block[..., None]), 0.0)
        grad_value = grad_value + jnp.einsum(
            "kgqn,qkgd->nkd",
            weights.astype(jnp.bfloat16),
            grad_block,
            preferred_element_type=jnp.float32,
        )
        grad_weights = jnp.einsum(
            "qkgd,nkd->kgqn", grad_block, own_values, preferred_element_type=jnp.float32
        )
        grad_scores = (weights * (grad_weights - delta_block[..., None])).astype(jnp.bfloat16)
        grad_key = grad_key + jnp.einsum(
            "kgqn,qkgd->nkd", grad_scores, query_block, preferred_element_type=jnp.float32
        )
        return ((grad_key, grad_value), None)

    outcome, ignored = lax.scan(
        block_step, carry, jnp.arange(piece_rows // block_rows, dtype=jnp.int32)
    )
    return outcome


def on_device(
    inputs, norm_gains, w_query, w_key, w_value, w_output, w_gate, w_up, w_down, cotangent
):
    ctx_size = lax.axis_size("ctx")
    device_count = lax.axis_size("dp") * ctx_size
    row_count = inputs.shape[2]
    seq_length = row_count * ctx_size
    first_row = lax.axis_index("ctx") * row_count
    key_block = min(512, seq_length)
    block_count = (first_row + row_count - 1) // key_block + 1
    group_size = H // KV
    cosine, sine_table = rope_tables(first_row + jnp.arange(row_count))
    weight_flats = (w_query, w_key, w_value, w_output, w_gate, w_up, w_down)
    piece_sizes = [flat_piece.shape[0] for flat_piece in weight_flats]
    packed = jnp.concatenate([flat_piece.reshape(1, -1) for flat_piece in weight_flats], axis=1)
    saved_rows = []
    out_rows = []
    grad_rows = []
    gain_terms = []
    for micro_batch in range(inputs.shape[0]):
        matrices = unpack(lax.all_gather(packed, ("dp", "ctx"), axis=0, tiled=True), piece_sizes)
        gain_rows = lax.all_gather(norm_gains, "ctx", axis=1, tiled=True)
        query_mat, key_mat, value_mat, output_mat, gate_mat, up_mat, down_mat = matrices
        x_float = inputs[micro_batch, 0].astype(jnp.float32)
        scale_one = rms_scale(x_float)
        normed_one = (x_float * scale_one * gain_rows[0]).astype(jnp.bfloat16)
        queries = (
            rotate(
                jnp.dot(normed_one, query_mat, preferred_element_type=jnp.float32),
                cosine,
                sine_table,
                H,
                1.0,
            )
            * score_scale
        ).astype(jnp.bfloat16)
        key_rows = rotate(
            jnp.dot(normed_one, key_mat, preferred_element_type=jnp.float32),
            cosine,
            sine_table,
            KV,
            1.0,
        ).astype(jnp.bfloat16)
        value_rows = jnp.dot(normed_one, value_mat, preferred_element_type=jnp.float32).astype(
            jnp.bfloat16
        )
        gathered_kv = lax.all_gather(
            jnp.concatenate([key_rows, value_rows], axis=1), "ctx", axis=0, tiled=True
        )
        attn_mixed, log_total = attend(queries, gathered_kv, first_row, key_block, block_count)
        attended = attn_mixed.astype(jnp.bfloat16)
        residual = x_float + jnp.dot(attended, output_mat, preferred_element_type=jnp.float32)
        scale_two = rms_scale(residual)
        normed_two = (residual * scale_two * gain_rows[1]).astype(jnp.bfloat16)
        gate_pre = jnp.dot(normed_two, gate_mat, preferred_element_type=jnp.float32)
        up_pre = jnp.dot(normed_two, up_mat, preferred_element_type=jnp.float32)
        gate_sig = jax.nn.sigmoid(gate_pre)
        swish_val = gate_pre * gate_sig
        activated = (swish_val * up_pre).astype(jnp.bfloat16)
        outcome = residual + jnp.dot(activated, down_mat, preferred_element_type=jnp.float32)
        out_rows.append(outcome.astype(jnp.bfloat16))
        query_back, key_back, value_back, output_back, gate_back, up_back, down_back = matrices
        grad_out = cotangent[micro_batch, 0]
        grad_act = against(grad_out, down_back)
        grad_gate_pre = (grad_act * up_pre * gate_sig * (1.0 + gate_pre * (1.0 - gate_sig))).astype(
            jnp.bfloat16
        )
        grad_up_pre = (grad_act * swish_val).astype(jnp.bfloat16)
        grad_norm_two = against(grad_gate_pre, gate_back) + against(grad_up_pre, up_back)
        gain_two = jnp.sum(grad_norm_two * residual * scale_two, axis=0)
        grad_residual = grad_out.astype(jnp.float32) + norm_back(
            grad_norm_two, residual, scale_two, gain_rows[1]
        )
        grad_branch = grad_residual.astype(jnp.bfloat16)
        grad_attn = against(grad_branch, output_back).astype(jnp.bfloat16)
        grad_grouped = grad_attn.reshape(row_count, KV, group_size, HD)
        product = (grad_attn.astype(jnp.float32) * attn_mixed).reshape(
            row_count, KV, group_size, HD
        )
        delta = jnp.transpose(jnp.sum(product, axis=-1), (1, 2, 0))
        grad_query = attend_back(
            queries, gathered_kv, first_row, key_block, block_count, log_total, grad_grouped, delta
        )
        stats = (
            lax.all_gather(log_total.reshape(H, row_count), "ctx", axis=1, tiled=True),
            lax.all_gather(delta.reshape(H, row_count), "ctx", axis=1, tiled=True),
        )
        own_keys = key_rows.reshape(row_count, KV, HD)
        own_values = value_rows.reshape(row_count, KV, HD)
        zero_rows = jnp.zeros((row_count, KV, HD), jnp.float32)
        grad_key_sum, grad_value_sum = key_side(
            own_keys,
            own_values,
            first_row,
            stats,
            (zero_rows, zero_rows),
            (
                lax.all_gather(queries, "ctx", axis=0, tiled=True),
                lax.all_gather(grad_attn, "ctx", axis=0, tiled=True),
            ),
        )
        grad_q_low = (rotate(grad_query, cosine, sine_table, H, -1.0) * score_scale).astype(
            jnp.bfloat16
        )
        grad_k_low = rotate(
            grad_key_sum.reshape(row_count, KV * HD), cosine, sine_table, KV, -1.0
        ).astype(jnp.bfloat16)
        grad_v_low = grad_value_sum.reshape(row_count, KV * HD).astype(jnp.bfloat16)
        grad_norm_one = (
            against(grad_q_low, query_back)
            + against(grad_k_low, key_back)
            + against(grad_v_low, value_back)
        )
        gain_one = jnp.sum(grad_norm_one * x_float * scale_one, axis=0)
        grad_x = grad_residual + norm_back(grad_norm_one, x_float, scale_one, gain_rows[0])
        grad_rows.append(grad_x.astype(jnp.bfloat16))
        gain_terms.append(jnp.stack([gain_one, gain_two], axis=0))
        saved_rows.append(
            (
                normed_one,
                grad_q_low,
                grad_k_low,
                grad_v_low,
                attended,
                grad_branch,
                normed_two,
                grad_gate_pre,
                grad_up_pre,
                activated,
                grad_out,
            )
        )
    joined = [
        jnp.concatenate([saved_set[member] for saved_set in saved_rows], axis=0)
        for member in range(11)
    ]
    local_grads = (
        across_rows(joined[0], joined[1]),
        across_rows(joined[0], joined[2]),
        across_rows(joined[0], joined[3]),
        across_rows(joined[4], joined[5]),
        across_rows(joined[6], joined[7]),
        across_rows(joined[6], joined[8]),
        across_rows(joined[9], joined[10]),
    )
    grad_table = jnp.concatenate(
        [grad_mat.reshape(device_count, -1) for grad_mat in local_grads], axis=1
    )
    owned = lax.psum_scatter(grad_table, ("dp", "ctx"), scatter_dimension=0, tiled=True)
    owned_parts = []
    offset = 0
    for piece_len in piece_sizes:
        owned_parts.append(owned[0, offset : offset + piece_len])
        offset = offset + piece_len
    gain_local = gain_terms[0]
    for extra_term in gain_terms[1:]:
        gain_local = gain_local + extra_term
    gain_total = lax.psum(gain_local, ("dp", "ctx"))
    gain_width = D // ctx_size
    gain_share = lax.dynamic_slice_in_dim(
        gain_total, lax.axis_index("ctx") * gain_width, gain_width, 1
    )
    return (
        jnp.stack(out_rows)[:, None],
        jnp.stack(grad_rows)[:, None],
        gain_share,
        owned_parts[0],
        owned_parts[1],
        owned_parts[2],
        owned_parts[3],
        owned_parts[4],
        owned_parts[5],
        owned_parts[6],
    )


def general_solution(mesh):
    placed = (
        P(None, "dp", "ctx", None),
        P(None, "ctx"),
        P(("dp", "ctx")),
        P(("dp", "ctx")),
        P(("dp", "ctx")),
        P(("dp", "ctx")),
        P(("dp", "ctx")),
        P(("dp", "ctx")),
        P(("dp", "ctx")),
        P(None, "dp", "ctx", None),
    )
    return jax.shard_map(
        on_device,
        mesh=mesh,
        in_specs=placed,
        out_specs=(
            P(None, "dp", "ctx", None),
            P(None, "dp", "ctx", None),
            P(None, "ctx"),
            P(("dp", "ctx")),
            P(("dp", "ctx")),
            P(("dp", "ctx")),
            P(("dp", "ctx")),
            P(("dp", "ctx")),
            P(("dp", "ctx")),
            P(("dp", "ctx")),
        ),
        check_vma=False,
    )


BF = jnp.bfloat16
F32 = jnp.float32
MESH = pl.DeviceIdType.MESH
MAIN = 16
PACK = 768


def place():
    dp_at = lax.axis_index("dp")
    ctx_at = lax.axis_index("ctx")
    core = lax.rem(ctx_at, 2)
    flip_one = dp_at + 1 - 2 * lax.rem(dp_at, 2)
    flip_two = lax.rem(dp_at + 2, 4)
    first = (1 - core) * flip_one + core * flip_two
    second = (1 - core) * flip_two + core * flip_one
    return (dp_at, ctx_at, core, ctx_at // 2, first, second, 3 - dp_at)


def greet(targets):
    barrier = pltpu.get_barrier_semaphore()
    for target in targets:
        pl.semaphore_signal(barrier, inc=1, device_id=target, device_id_type=MESH)
    pl.semaphore_wait(barrier, len(targets))


def rows(index, size):
    return pl.ds(pl.multiple_of(index * size, size), size)


def remote(src, dst, send, recv, target):
    return pltpu.make_async_remote_copy(
        src_ref=src, dst_ref=dst, send_sem=send, recv_sem=recv, device_id=target, device_id_type=MESH
    )


def tail_matrix(shards, transposed):
    width = shards * MAIN
    shape = (width, 384) if transposed else (384, width)
    out_at = lax.broadcasted_iota(jnp.int32, shape, 1 if transposed else 0)
    in_at = lax.broadcasted_iota(jnp.int32, shape, 0 if transposed else 1)
    wanted = (lax.rem(out_at, 64) // 2) * MAIN + (out_at // 64) * 2 + lax.rem(out_at, 2)
    return jnp.where(wanted == in_at, 1.0, 0.0).astype(BF)


def view(ref, index, size):
    if len(ref.shape) == 3:
        return ref.at[:, rows(index, size), :]
    return ref.at[rows(index, size), :]


def vmem_specs(count):
    return [pl.BlockSpec(memory_space=pltpu.VMEM)] * count


def comm_params(number):
    return pltpu.CompilerParams(
        collective_id=number, has_side_effects=True, vmem_limit_bytes=56 * 1024 * 1024
    )


class WeightGather:
    def __init__(self, ctx_size, refs, sizes, send, recv):
        self.ctx_size = ctx_size
        self.refs = refs
        self.sizes = sizes
        self.send = send
        self.recv = recv
        self.sent = []
        dp_at, ctx_at, core, z_at, first, second, across = place()
        self.at = (dp_at, first, second, across)
        self.core = core
        depth = ctx_size // 2
        self.me = dp_at * ctx_size + ctx_at
        self.sibling = (dp_at, ctx_at + 1 - 2 * core)
        self.to_first = (first, ctx_at)
        self.to_second = (second, ctx_at)
        self.z_peers = [(dp_at, 2 * lax.rem(z_at + i, depth) + core) for i in range(1, depth)]
        self.back = [lax.rem(z_at + depth - i, depth) for i in range(depth)]
        self.targets = self.z_peers + [self.to_first, self.to_second, self.sibling]

    def copies(self, shard, target, slot):
        return [
            remote(
                view(ref, shard, size),
                view(ref, shard, size),
                self.send.at[slot, k],
                self.recv.at[shard, k],
                target,
            )
            for k, (ref, size) in enumerate(zip(self.refs, self.sizes))
        ]

    def push(self, shard, targets):
        for target in targets:
            group = self.copies(shard, target, len(self.sent))
            for one in group:
                one.start()
            self.sent.append(group)

    def arrive(self, shard):
        for one in self.copies(shard, self.sibling, 0):
            one.wait_recv()

    def begin(self):
        self.push(self.me, self.targets)

    def pass_on(self, shard, targets):
        self.arrive(shard)
        self.push(shard, targets)

    def along_z(self):
        for z_from in self.back[1:]:
            shard = self.at[0] * self.ctx_size + 2 * z_from + self.core
            self.pass_on(shard, [self.to_first, self.to_second, self.sibling])

    def across_dp(self, z_from):
        shard = self.at[1] * self.ctx_size + 2 * z_from + self.core
        self.pass_on(shard, [self.to_second, self.sibling])
        shard = self.at[2] * self.ctx_size + 2 * z_from + self.core
        self.pass_on(shard, [self.sibling])

    def corner(self, z_from):
        self.pass_on(self.at[3] * self.ctx_size + 2 * z_from + self.core, [self.sibling])

    def finish(self):
        for dp_from in self.at:
            for z_from in self.back:
                self.arrive(dp_from * self.ctx_size + 2 * z_from + 1 - self.core)
        for group in self.sent:
            for one in group:
                one.wait_send()


def gather_first_kernel(
    ctx_size,
    w_ref,
    t_ref,
    f_ref,
    d_ref,
    ow_ref,
    ox_ref,
    og_ref,
    lf_ref,
    ld_ref,
    tg_ref,
    send,
    recv,
    send_l,
    recv_l,
):
    shards = 4 * ctx_size
    plan = WeightGather(ctx_size, (ow_ref, tg_ref), (16, 16), send, recv)
    greet(plan.targets)
    ow_ref[rows(plan.me, 16), :] = w_ref[...]
    tg_ref[rows(plan.me, 16), :] = t_ref[...]
    z_at = plan.back[0]
    lf_ref[:, rows(z_at, 16), :] = f_ref[...]
    ld_ref[rows(z_at, 48), :] = d_ref[...]
    plan.begin()
    sent = []

    def line(z_from, target, slot):
        return [
            remote(view(ref, z_from, size), view(ref, z_from, size), send_l.at[slot, k], recv_l.at[z_from, k], target)
            for k, (ref, size) in enumerate(((lf_ref, 16), (ld_ref, 48)))
        ]

    for slot, target in enumerate(plan.z_peers):
        group = line(z_at, target, slot)
        for one in group:
            one.start()
        sent.append(group)
    plan.along_z()
    for z_from in plan.back:
        plan.across_dp(z_from)
    for z_from in plan.back:
        plan.corner(z_from)
    plan.finish()
    for z_from in plan.back[1:]:
        for one in line(z_from, plan.sibling, 0):
            one.wait_recv()
    for group in sent:
        for one in group:
            one.wait_send()
    unpacked = jnp.dot(
        tail_matrix(shards, False), tg_ref[...], preferred_element_type=F32
    ).astype(BF)
    for part in range(6):
        piece = unpacked[64 * part : 64 * part + 64]
        columns = slice((part % 2) * PACK, (part % 2 + 1) * PACK)
        if part < 2:
            ow_ref[512:576, columns] = piece
        else:
            ox_ref[part // 2 - 1, :, columns] = piece
    og_ref[...] = tg_ref[0 : ctx_size * 16, :]


def gather_first(ctx_size, w_main, w_tail, w_ffn, w_low):
    shards = 4 * ctx_size
    depth = ctx_size // 2
    return pl.pallas_call(
        functools.partial(gather_first_kernel, ctx_size),
        out_shape=(
            jax.ShapeDtypeStruct((D, FF), BF),
            jax.ShapeDtypeStruct((2, 64, FF), BF),
            jax.ShapeDtypeStruct((ctx_size * 16, PACK), BF),
            jax.ShapeDtypeStruct((2, depth * 16, FF), BF),
            jax.ShapeDtypeStruct((depth * 48, D), BF),
        ),
        in_specs=vmem_specs(4),
        out_specs=tuple(vmem_specs(5)),
        scratch_shapes=[
            pltpu.VMEM((shards * 16, PACK), BF),
            pltpu.SemaphoreType.DMA((shards, 2)),
            pltpu.SemaphoreType.DMA((shards, 2)),
            pltpu.SemaphoreType.DMA((depth, 2)),
            pltpu.SemaphoreType.DMA((depth, 2)),
        ],
        compiler_params=comm_params(0),
        name="gather_first",
    )(w_main, w_tail, w_ffn, w_low)


def head_rows(ref, micro, group, row_count):
    return jnp.concatenate(
        [
            ref[micro * row_count : (micro + 1) * row_count, HD * h : HD * h + HD]
            for h in range(3 * group, 3 * group + 3)
        ],
        axis=0,
    )


def attend_forward_kernel(
    ctx_size,
    w_ref,
    d_ref,
    x_ref,
    q_ref,
    kv_ref,
    ow_ref,
    od_ref,
    kvg_ref,
    mixed_ref,
    lse_ref,
    send,
    recv,
    send_t,
    recv_t,
):
    plan = WeightGather(ctx_size, (ow_ref, od_ref), (16, 48), send, recv)
    ctx_at = lax.axis_index("ctx")
    tokens = q_ref.shape[0]
    row_count = tokens // 2
    seq_length = ctx_size * row_count
    first_row = ctx_at * row_count
    core = plan.core
    greet(plan.targets)
    kvg_ref[ctx_at] = kv_ref[...]
    sent = []

    def push(ctx_from, targets):
        for target in targets:
            part = kvg_ref.at[ctx_from]
            one = remote(part, part, send_t.at[len(sent)], recv_t.at[ctx_from], target)
            one.start()
            sent.append(one)

    def arrive(ctx_from):
        part = kvg_ref.at[ctx_from]
        remote(part, part, send_t.at[0], recv_t.at[ctx_from], plan.sibling).wait_recv()

    push(ctx_at, plan.z_peers + [plan.sibling])
    for z_from in range(ctx_size // 2):
        shard = plan.at[0] * ctx_size + 2 * z_from + core
        ow_ref[:, rows(shard, 16), :] = w_ref[:, 16 * z_from : 16 * z_from + 16, :]
        od_ref[rows(shard, 48), :] = d_ref[48 * z_from : 48 * z_from + 48, :]
        plan.push(shard, [plan.to_first, plan.to_second, plan.sibling])
    ow_ref[:, 512:576, :] = x_ref[...]
    for z_from in plan.back[1:]:
        arrive(2 * z_from + core)
        push(2 * z_from + core, [plan.sibling])
    for z_from in plan.back:
        arrive(2 * z_from + 1 - core)
    services = [functools.partial(plan.across_dp, z_from) for z_from in range(ctx_size // 2)]
    shape = (3 * row_count, seq_length)
    query_pos = first_row + lax.rem(lax.broadcasted_iota(jnp.int32, shape, 0), row_count)
    visible = lax.broadcasted_iota(jnp.int32, shape, 1) <= query_pos
    lanes = lax.broadcasted_iota(jnp.int32, (row_count, 128), 1)
    for micro in range(2):
        spot = slice(micro * row_count, (micro + 1) * row_count)
        logs = jnp.zeros((row_count, 128), F32)
        for group in range(KV):
            queries = head_rows(q_ref, micro, group, row_count)
            keys = kvg_ref[:, spot, HD * group : HD * group + HD].reshape(seq_length, HD)
            low = KV * HD + HD * group
            values = kvg_ref[:, spot, low : low + HD].reshape(seq_length, HD)
            scores = jnp.where(visible, against(queries, keys), big_negative)
            top = jnp.max(scores, axis=-1, keepdims=True)
            raised = jnp.exp(scores - top)
            total = jnp.sum(raised, axis=-1, keepdims=True)
            probs_low = (raised * (1.0 / total)).astype(BF)
            mixed = jnp.dot(probs_low, values, preferred_element_type=F32)
            log_total = top + jnp.log(total)
            for member in range(3):
                h = 3 * group + member
                part = slice(member * row_count, (member + 1) * row_count)
                mixed_ref[spot, HD * h : HD * h + HD] = mixed[part]
                logs = jnp.where(lanes == h, log_total[part], logs)
            if services:
                services.pop(0)()
        lse_ref[spot, :] = logs
    for service in services:
        service()
    for z_from in plan.back:
        plan.corner(z_from)
    plan.finish()
    for one in sent:
        one.wait_send()


def attend_forward(ctx_size, w_main, w_low, w_extra, queries, kv_rows):
    shards = 4 * ctx_size
    tokens = queries.shape[0]
    return pl.pallas_call(
        functools.partial(attend_forward_kernel, ctx_size),
        out_shape=(
            jax.ShapeDtypeStruct((2, D, FF), BF),
            jax.ShapeDtypeStruct((FF, D), BF),
            jax.ShapeDtypeStruct((ctx_size,) + kv_rows.shape, BF),
            jax.ShapeDtypeStruct((tokens, H * HD), F32),
            jax.ShapeDtypeStruct((tokens, 128), F32),
        ),
        in_specs=vmem_specs(5),
        out_specs=tuple(vmem_specs(5)),
        scratch_shapes=[
            pltpu.SemaphoreType.DMA((shards, 2)),
            pltpu.SemaphoreType.DMA((shards, 2)),
            pltpu.SemaphoreType.DMA((ctx_size,)),
            pltpu.SemaphoreType.DMA((ctx_size,)),
        ],
        compiler_params=comm_params(1),
        name="attend_forward",
    )(w_main, w_low, w_extra, queries, kv_rows)


class GradScatter:
    def __init__(self, ctx_size, own, sizes, slots, sems):
        self.own = own
        self.sizes = sizes
        count = len(own)
        self.paired, self.via, self.from_first, self.from_second, self.along = [
            slots[k * count : (k + 1) * count] for k in range(5)
        ]
        self.send_c, self.recv_c, self.send_d, self.recv_d, self.send_z, self.recv_z = sems
        self.ctx_size = ctx_size
        self.depth = ctx_size // 2
        dp_at, ctx_at, core, z_at, first, second, across = place()
        self.at = (dp_at, first, second, across)
        self.core = core
        self.z_at = z_at
        self.sibling = (dp_at, ctx_at + 1 - 2 * core)
        self.to_first = (first, ctx_at)
        self.to_second = (second, ctx_at)
        self.order = [lax.rem(z_at + i, self.depth) for i in range(1, self.depth + 1)]
        self.z_peers = [(dp_at, 2 * z_to + core) for z_to in self.order[:-1]]
        self.targets = self.z_peers + [self.to_first, self.to_second, self.sibling]
        self.sent = []

    def views(self, refs, index):
        return [view(ref, index, size) for ref, size in zip(refs, self.sizes)]

    def ship(self, src, dst, send, recv, target):
        group = [
            remote(src[k], dst[k], send.at[k], recv.at[k], target) for k in range(len(src))
        ]
        for one in group:
            one.start()
        self.sent.append(group)

    def arrive(self, dst, recv):
        for k in range(len(dst)):
            remote(dst[k], dst[k], recv.at[k], recv.at[k], self.sibling).wait_recv()

    def add(self, dst, terms):
        for k in range(len(dst)):
            total = dst[k][...].astype(F32)
            for term in terms:
                total = total + term[k][...].astype(F32)
            dst[k][...] = total.astype(BF)

    def begin(self):
        dp_at, first, second, across = self.at
        for z_to in self.order:
            for dp_to in (across, second, first, dp_at):
                shard = dp_to * self.ctx_size + 2 * z_to + 1 - self.core
                slot = dp_to * self.depth + z_to
                self.ship(
                    self.views(self.own, shard),
                    self.views(self.paired, slot),
                    self.send_c.at[slot],
                    self.recv_c.at[slot],
                    self.sibling,
                )

    def pair_up(self, dp_to, z_to):
        slot = dp_to * self.depth + z_to
        partial = self.views(self.paired, slot)
        self.arrive(partial, self.recv_c.at[slot])
        self.add(
            partial, [self.views(self.own, dp_to * self.ctx_size + 2 * z_to + self.core)]
        )
        return partial

    def leave(self, partial, slots, kind, z_to, target):
        self.ship(
            partial,
            self.views(slots, z_to),
            self.send_d.at[kind, z_to],
            self.recv_d.at[kind, z_to],
            target,
        )

    def pairs(self, z_to):
        dp_at, first, second, across = self.at
        self.leave(self.pair_up(across, z_to), self.via, 0, z_to, self.to_second)
        self.leave(self.pair_up(second, z_to), self.from_second, 1, z_to, self.to_second)
        self.pair_up(first, z_to)
        self.pair_up(dp_at, z_to)

    def relay(self, z_to):
        partial = self.views(self.paired, self.at[1] * self.depth + z_to)
        came = self.views(self.via, z_to)
        self.arrive(came, self.recv_d.at[0, z_to])
        self.add(partial, [came])
        self.leave(partial, self.from_first, 2, z_to, self.to_first)

    def gathered(self, number):
        z_to = self.order[number]
        partial = self.views(self.paired, self.at[0] * self.depth + z_to)
        ahead = self.views(self.from_second, z_to)
        aside = self.views(self.from_first, z_to)
        self.arrive(ahead, self.recv_d.at[1, z_to])
        self.arrive(aside, self.recv_d.at[2, z_to])
        self.add(partial, [ahead, aside])
        if number < self.depth - 1:
            self.ship(
                partial,
                self.views(self.along, self.z_at),
                self.send_z.at[z_to],
                self.recv_z.at[self.z_at],
                (self.at[0], 2 * z_to + self.core),
            )

    def finish(self, outs):
        for z_from in self.order[:-1]:
            self.arrive(self.views(self.along, z_from), self.recv_z.at[z_from])
        mine = self.views(self.paired, self.at[0] * self.depth + self.z_at)
        others = [self.views(self.along, z_from) for z_from in self.order[:-1]]
        for k, out in enumerate(outs):
            total = mine[k][...].astype(F32)
            for other in others:
                total = total + other[k][...].astype(F32)
            out[...] = total
        for group in self.sent:
            for one in group:
                one.wait_send()


def scatter_scratch(ctx_size, shapes):
    depth = ctx_size // 2
    slots = []
    for count in (4 * depth, depth, depth, depth, depth):
        for shape in shapes:
            slots.append(pltpu.VMEM(shape[:-2] + (count * shape[-2], shape[-1]), BF))
    kinds = len(shapes)
    pairs = [(4 * depth, kinds), (3, depth, kinds), (depth, kinds)]
    return slots + [pltpu.SemaphoreType.DMA(pair) for pair in pairs for twice in range(2)]


def attend_backward_kernel(
    ctx_size,
    gw_ref,
    gd_ref,
    q_ref,
    kvg_ref,
    ga_ref,
    mixed_ref,
    lse_ref,
    ow_ref,
    od_ref,
    dq_ref,
    dkv_ref,
    parts_ref,
    paired_t,
    along_t,
    send_c,
    recv_c,
    send_z,
    recv_z,
    *scratch
):
    plan = GradScatter(ctx_size, (gw_ref, gd_ref), (16, 48), scratch[:10], scratch[10:])
    ctx_at = lax.axis_index("ctx")
    tokens = q_ref.shape[0]
    row_count = tokens // 2
    seq_length = ctx_size * row_count
    first_row = ctx_at * row_count
    core = plan.core
    greet(plan.targets)
    plan.begin()
    sent = []

    def swap_pairs(micro):
        spot = slice(micro * row_count, (micro + 1) * row_count)
        for z_to in plan.order:
            one = remote(
                parts_ref.at[2 * z_to + 1 - core, spot],
                paired_t.at[z_to, spot],
                send_c.at[micro, z_to],
                recv_c.at[micro, z_to],
                plan.sibling,
            )
            one.start()
            sent.append(one)

    def pass_pairs(micro):
        spot = slice(micro * row_count, (micro + 1) * row_count)
        for number, z_to in enumerate(plan.order):
            part = paired_t.at[z_to, spot]
            remote(
                part, part, send_c.at[micro, z_to], recv_c.at[micro, z_to], plan.sibling
            ).wait_recv()
            part[...] = (
                part[...].astype(F32) + parts_ref[2 * z_to + core, spot].astype(F32)
            ).astype(BF)
            if number < plan.depth - 1:
                one = remote(
                    part,
                    along_t.at[plan.z_at, spot],
                    send_z.at[micro, z_to],
                    recv_z.at[micro, plan.z_at],
                    (plan.at[0], 2 * z_to + core),
                )
                one.start()
                sent.append(one)

    services = [functools.partial(plan.pairs, z_to) for z_to in plan.order]
    services = services + [functools.partial(plan.relay, z_to) for z_to in plan.order]
    shape = (seq_length, 3 * row_count)
    query_pos = first_row + lax.rem(lax.broadcasted_iota(jnp.int32, shape, 1), row_count)
    visible = lax.broadcasted_iota(jnp.int32, shape, 0) <= query_pos
    lanes = lax.broadcasted_iota(jnp.int32, (row_count, 128), 1)
    for micro in range(2):
        spot = slice(micro * row_count, (micro + 1) * row_count)
        deltas = jnp.zeros((row_count, 128), F32)
        for h in range(H):
            columns = slice(HD * h, HD * h + HD)
            product = ga_ref[spot, columns].astype(F32) * mixed_ref[spot, columns]
            deltas = jnp.where(lanes == h, jnp.sum(product, axis=-1, keepdims=True), deltas)
        deltas = deltas.T
        logs = lse_ref[spot, :].T
        for group in range(KV):
            queries = head_rows(q_ref, micro, group, row_count)
            grads = head_rows(ga_ref, micro, group, row_count)
            low = KV * HD + HD * group
            keys = kvg_ref[:, spot, HD * group : HD * group + HD].reshape(seq_length, HD)
            values = kvg_ref[:, spot, low : low + HD].reshape(seq_length, HD)
            log_row = jnp.concatenate(
                [logs[h : h + 1] for h in range(3 * group, 3 * group + 3)], axis=1
            )
            delta_row = jnp.concatenate(
                [deltas[h : h + 1] for h in range(3 * group, 3 * group + 3)], axis=1
            )
            scores = jnp.where(visible, against(keys, queries), big_negative)
            probs = jnp.exp(scores - log_row)
            grad_value = jnp.dot(probs.astype(BF), grads, preferred_element_type=F32)
            grad_scores = (probs * (against(values, grads) - delta_row)).astype(BF)
            grad_key = jnp.dot(grad_scores, queries, preferred_element_type=F32)
            grad_query = across_rows(keys, grad_scores).T
            parts_ref[:, spot, HD * group : HD * group + HD] = grad_key.astype(BF).reshape(
                ctx_size, row_count, HD
            )
            parts_ref[:, spot, low : low + HD] = grad_value.astype(BF).reshape(
                ctx_size, row_count, HD
            )
            for member in range(3):
                h = 3 * group + member
                dq_ref[spot, HD * h : HD * h + HD] = grad_query[
                    member * row_count : (member + 1) * row_count
                ]
            if services:
                services.pop(0)()
            if micro == 1 and group == 0:
                pass_pairs(0)
        swap_pairs(micro)
    for service in services:
        service()
    pass_pairs(1)
    for number in range(plan.depth):
        plan.gathered(number)
    total = paired_t[plan.z_at].astype(F32)
    for z_from in plan.order[:-1]:
        for micro in range(2):
            part = along_t.at[z_from, micro * row_count : (micro + 1) * row_count]
            remote(
                part, part, send_z.at[micro, z_from], recv_z.at[micro, z_from], plan.sibling
            ).wait_recv()
        total = total + along_t[z_from].astype(F32)
    dkv_ref[...] = total
    plan.finish((ow_ref, od_ref))
    for one in sent:
        one.wait_send()


def attend_backward(ctx_size, grad_main, grad_low, queries, kvg, grad_attn, mixed, lse):
    depth = ctx_size // 2
    tokens, width = kvg.shape[1:]
    return pl.pallas_call(
        functools.partial(attend_backward_kernel, ctx_size),
        out_shape=(
            jax.ShapeDtypeStruct((2, 16, FF), F32),
            jax.ShapeDtypeStruct((48, D), F32),
            jax.ShapeDtypeStruct((tokens, H * HD), F32),
            jax.ShapeDtypeStruct((tokens, width), F32),
        ),
        in_specs=vmem_specs(7),
        out_specs=tuple(vmem_specs(4)),
        scratch_shapes=[
            pltpu.VMEM((ctx_size, tokens, width), BF),
            pltpu.VMEM((depth, tokens, width), BF),
            pltpu.VMEM((depth, tokens, width), BF),
        ]
        + [pltpu.SemaphoreType.DMA((2, depth))] * 4
        + scatter_scratch(ctx_size, ((2, 16, FF), (48, D))),
        compiler_params=comm_params(2),
        name="attend_backward",
    )(grad_main, grad_low, queries, kvg, grad_attn, mixed, lse)


def scatter_last_kernel(ctx_size, gw_ref, ge_ref, gx_ref, ow_ref, ot_ref, tail, *scratch):
    plan = GradScatter(ctx_size, (gw_ref, tail), (16, 16), scratch[:10], scratch[10:])
    greet(plan.targets)
    pieces = []
    for part in range(6):
        columns = slice((part % 2) * PACK, (part % 2 + 1) * PACK)
        if part < 2:
            pieces.append(gw_ref[512:576, columns])
        else:
            pieces.append(ge_ref[part // 2 - 1, :, columns])
    stacked = jnp.concatenate(pieces, axis=0)
    spread = jnp.dot(tail_matrix(4 * ctx_size, True), stacked, preferred_element_type=F32)
    for block in range(4):
        part = slice(block * ctx_size * 16, (block + 1) * ctx_size * 16)
        tail[part, :] = (spread[part] + gx_ref[...].astype(F32)).astype(BF)
    plan.begin()
    for z_to in plan.order:
        plan.pairs(z_to)
    for z_to in plan.order:
        plan.relay(z_to)
    for number in range(plan.depth):
        plan.gathered(number)
    plan.finish((ow_ref, ot_ref))


def scatter_last(ctx_size, grad_main, grad_extra, gain_rows):
    return pl.pallas_call(
        functools.partial(scatter_last_kernel, ctx_size),
        out_shape=(
            jax.ShapeDtypeStruct((16, FF), F32),
            jax.ShapeDtypeStruct((16, PACK), F32),
        ),
        in_specs=vmem_specs(3),
        out_specs=tuple(vmem_specs(2)),
        scratch_shapes=[pltpu.VMEM((4 * ctx_size * 16, PACK), BF)]
        + scatter_scratch(ctx_size, ((16, FF), (16, PACK))),
        compiler_params=comm_params(3),
        name="scatter_last",
    )(grad_main, grad_extra, gain_rows)


def dot(left, right):
    return jnp.dot(left, right, preferred_element_type=F32)


def shuffle_matrix(shards):
    natural = lax.broadcasted_iota(jnp.int32, (D, D), 0)
    moved = lax.broadcasted_iota(jnp.int32, (D, D), 1)
    owner = natural // 18
    within = natural % 18
    wanted = jnp.where(within < MAIN, owner * MAIN + within, 512 + owner * 2 + within - MAIN)
    return jnp.where(wanted == moved, 1.0, 0.0).astype(BF)


def put_back(values, shuffle):
    upper = lax.reduce_precision(values, 8, 7)
    return against(upper.astype(BF), shuffle) + against((values - upper).astype(BF), shuffle)


def split_tail(w_query, w_key, w_value, w_output, w_gate, w_up):
    mats = [flat.reshape(18, -1) for flat in (w_query, w_key, w_output, w_value)]
    first_slab = jnp.concatenate(mats, axis=1)
    slabs = jnp.stack([first_slab, w_gate.reshape(18, FF), w_up.reshape(18, FF)])
    tail = slabs[:, MAIN:, :].reshape(3, 2, 2, PACK).transpose(0, 2, 1, 3).reshape(12, PACK)
    return (slabs[:, :MAIN, :], tail)


def fast_device(
    inputs, norm_gains, w_query, w_key, w_value, w_output, w_gate, w_up, w_down, cotangent
):
    ctx_size = lax.axis_size("ctx")
    shards = 4 * ctx_size
    micro = inputs.shape[0]
    row_count = inputs.shape[2]
    tokens = micro * row_count
    first_row = lax.axis_index("ctx") * row_count
    gain_width = D // ctx_size
    main, tail = split_tail(w_query, w_key, w_value, w_output, w_gate, w_up)
    gain_parts = []
    left = norm_gains
    for step in range(3):
        piece = lax.reduce_precision(left, 8, 7)
        gain_parts.append(piece)
        left = left - piece
    gain_rows = jnp.pad(
        jnp.stack(gain_parts), ((0, 1), (0, 0), (0, PACK // 2 - gain_width))
    ).reshape(4, PACK)
    tail = jnp.concatenate([tail, gain_rows.astype(BF)], axis=0)
    attn_mats, tail_rows, gain_blocks, line_ffn, line_low = gather_first(
        ctx_size, main[0], tail, main[1:], w_down.reshape(48, D)
    )
    gain_blocks = gain_blocks.reshape(ctx_size, 16, 2, PACK // 2)[:, 12:15, :, :gain_width]
    gains = (
        jnp.sum(gain_blocks.astype(F32), axis=1).transpose(1, 0, 2).reshape(2, D)
    )
    query_mat = attn_mats[:, 0:576]
    key_mat = attn_mats[:, 576:768]
    output_mat = attn_mats[:, 768:1344]
    value_mat = attn_mats[:, 1344:1536]
    shuffle = shuffle_matrix(shards)
    cosine, sine_table = rope_tables(first_row + jnp.arange(row_count))
    cosine = jnp.concatenate([cosine] * micro, axis=0)
    sine_table = jnp.concatenate([sine_table] * micro, axis=0)
    x_float = inputs.reshape(tokens, D).astype(F32)
    grad_out = cotangent.reshape(tokens, D)
    scale_one = rms_scale(x_float)
    normed_one = dot((x_float * scale_one * gains[0]).astype(BF), shuffle).astype(BF)
    queries = (
        rotate(dot(normed_one, query_mat), cosine, sine_table, H, 1.0) * score_scale
    ).astype(BF)
    key_rows = rotate(dot(normed_one, key_mat), cosine, sine_table, KV, 1.0).astype(BF)
    value_rows = dot(normed_one, value_mat).astype(BF)
    ffn_mats, down_mat, gathered, mixed, log_total = attend_forward(
        ctx_size,
        line_ffn,
        line_low,
        tail_rows,
        queries,
        jnp.concatenate([key_rows, value_rows], axis=1),
    )
    gate_mat = ffn_mats[0]
    up_mat = ffn_mats[1]
    attended = dot(mixed.astype(BF), shuffle).astype(BF)
    residual = x_float + dot(attended, output_mat)
    scale_two = rms_scale(residual)
    normed_two = dot((residual * scale_two * gains[1]).astype(BF), shuffle).astype(BF)
    gate_pre = dot(normed_two, gate_mat)
    up_pre = dot(normed_two, up_mat)
    gate_sig = jax.nn.sigmoid(gate_pre)
    swish_val = gate_pre * gate_sig
    activated = (swish_val * up_pre).astype(BF)
    outcome = residual + dot(activated, down_mat)
    grad_act = against(grad_out, down_mat)
    grad_gate_pre = (grad_act * up_pre * gate_sig * (1.0 + gate_pre * (1.0 - gate_sig))).astype(BF)
    grad_up_pre = (grad_act * swish_val).astype(BF)
    grad_norm_two = put_back(
        against(grad_gate_pre, gate_mat) + against(grad_up_pre, up_mat), shuffle
    )
    gain_two = jnp.sum(grad_norm_two * residual * scale_two, axis=0)
    grad_residual = grad_out.astype(F32) + norm_back(grad_norm_two, residual, scale_two, gains[1])
    grad_branch = grad_residual.astype(BF)
    grad_attn = against(against(grad_branch, output_mat).astype(BF), shuffle).astype(BF)
    grad_ffn = jnp.stack(
        [across_rows(normed_two, grad_gate_pre), across_rows(normed_two, grad_up_pre)]
    ).astype(BF)
    grad_low = across_rows(activated, grad_out).astype(BF)
    own_ffn, own_low, grad_query, summed = attend_backward(
        ctx_size, grad_ffn, grad_low, queries, gathered, grad_attn, mixed, log_total
    )
    grad_q_low = (rotate(grad_query, cosine, sine_table, H, -1.0) * score_scale).astype(BF)
    grad_k_low = rotate(summed[:, : KV * HD], cosine, sine_table, KV, -1.0).astype(BF)
    grad_v_low = summed[:, KV * HD :].astype(BF)
    grad_norm_one = put_back(
        against(grad_q_low, query_mat)
        + against(grad_k_low, key_mat)
        + against(grad_v_low, value_mat),
        shuffle,
    )
    gain_one = jnp.sum(grad_norm_one * x_float * scale_one, axis=0)
    grad_x = grad_residual + norm_back(grad_norm_one, x_float, scale_one, gains[0])
    grad_first = jnp.concatenate(
        [
            across_rows(normed_one, grad_q_low),
            across_rows(normed_one, grad_k_low),
            across_rows(attended, grad_branch),
            across_rows(normed_one, grad_v_low),
        ],
        axis=1,
    ).astype(BF)
    gain_local = jnp.stack([gain_one, gain_two]).reshape(2, ctx_size, gain_width)
    gain_pack = jnp.pad(
        gain_local.transpose(1, 0, 2), ((0, 0), (0, 0), (0, PACK // 2 - gain_width))
    ).reshape(ctx_size, 1, PACK)
    gain_pack = jnp.pad(gain_pack, ((0, 0), (12, 3), (0, 0))).reshape(ctx_size * 16, PACK)
    own_first, own_tail = scatter_last(
        ctx_size, grad_first, grad_ffn[:, 512:576], gain_pack.astype(BF)
    )
    own_main = jnp.concatenate([own_first[None], own_ffn], axis=0)
    tail_rows = own_tail[:12].reshape(3, 2, 2, PACK).transpose(0, 2, 1, 3).reshape(3, 2, FF)
    owned = jnp.concatenate([own_main, tail_rows], axis=1)
    gain_share = own_tail[12].reshape(2, PACK // 2)[:, :gain_width]
    shape_out = inputs.shape
    return (
        outcome.astype(BF).reshape(shape_out),
        grad_x.astype(BF).reshape(shape_out),
        gain_share,
        owned[0, :, 0:576].reshape(-1),
        owned[0, :, 576:768].reshape(-1),
        owned[0, :, 1344:1536].reshape(-1),
        owned[0, :, 768:1344].reshape(-1),
        owned[1].reshape(-1),
        owned[2].reshape(-1),
        own_low.reshape(-1),
    )


def solution(mesh):
    sizes = dict(mesh.shape)
    if sizes["dp"] != 4 or sizes["ctx"] % 2 or sizes["dp"] * sizes["ctx"] * 18 != D:
        return general_solution(mesh)
    tokens_spec = P(None, "dp", "ctx", None)
    flat_spec = P(("dp", "ctx"))
    return jax.shard_map(
        fast_device,
        mesh=mesh,
        in_specs=(tokens_spec, P(None, "ctx")) + (flat_spec,) * 7 + (tokens_spec,),
        out_specs=(tokens_spec, tokens_spec, P(None, "ctx")) + (flat_spec,) * 7,
        check_vma=False,
    )
```
